128 devices in a mesh: dp: 64 (over z, x, y_lo, core), blk: 2 (over y_hi).
Axes of the slice: x: 4, y: 4 (y_hi: 2, y_lo: 2; y = y_hi * 2 + y_lo), z: 4, core: 2. Of those that a mesh axis runs over, the one named last changes fastest.
Arguments:
- inputs: bfloat16 [64, 256, 1152], P('dp', 'blk'), may hold values from -6 to 6
- text: bfloat16 [64, 32, 4096], P('dp', 'blk'), may hold values from -6 to 6
- masked: int32 [64, 256], P('dp', 'blk'), may hold values from 0 to 1, as said below
- cot: bfloat16 [64, 256, 1152], P('dp', 'blk'), may hold values from -6 to 6
- norm_gains: bfloat16 [3, 1152], P(None, ('dp', 'blk')), may hold values from 0.5 to 1.5
- norm_biases: bfloat16 [3, 1152], P(None, ('dp', 'blk')), may hold values from -2 to 2
- w_qkv: bfloat16 [1152, 3456], P(('dp', 'blk')), may hold values from -0.1875 to 0.1875
- w_out: bfloat16 [1152, 1152], P(('dp', 'blk')), may hold values from -0.75 to 0.75
- w_text: bfloat16 [4096, 1152], P(('dp', 'blk')), may hold values from -0.09375 to 0.09375
- w_query: bfloat16 [1152, 1152], P(('dp', 'blk')), may hold values from -0.1875 to 0.1875
- w_memory: bfloat16 [1152, 2304], P(('dp', 'blk')), may hold values from -0.1875 to 0.1875
- w_cross_out: bfloat16 [1152, 1152], P(('dp', 'blk')), may hold values from -0.375 to 0.375
- w_up: bfloat16 [1152, 4608], P(('dp', 'blk')), may hold values from -0.1875 to 0.1875
- up_bias: bfloat16 [4608], P(('dp', 'blk')), may hold values from -2 to 2
- w_down: bfloat16 [4608, 1152], P(('dp', 'blk')), may hold values from -0.09375 to 0.09375
- down_bias: bfloat16 [1152], P(('dp', 'blk')), may hold values from -2 to 2
Outputs:
- block_output: bfloat16 [64, 256, 1152], P('dp', 'blk')
- input_grads: float32 [64, 256, 1152], P('dp', 'blk')
- norm_gains_grad: float32 [3, 1152], P(None, ('dp', 'blk'))
- norm_biases_grad: float32 [3, 1152], P(None, ('dp', 'blk'))
- w_qkv_grad: float32 [1152, 3456], P(('dp', 'blk'))
- w_out_grad: float32 [1152, 1152], P(('dp', 'blk'))
- w_text_grad: float32 [4096, 1152], P(('dp', 'blk'))
- w_query_grad: float32 [1152, 1152], P(('dp', 'blk'))
- w_memory_grad: float32 [1152, 2304], P(('dp', 'blk'))
- w_cross_out_grad: float32 [1152, 1152], P(('dp', 'blk'))
- w_up_grad: float32 [1152, 4608], P(('dp', 'blk'))
- up_bias_grad: float32 [4608], P(('dp', 'blk'))
- w_down_grad: float32 [4608, 1152], P(('dp', 'blk'))
- down_bias_grad: float32 [1152], P(('dp', 'blk'))
The draws below stay inside these ranges and needn't reach their ends.
Inputs may be any that keep to these rules, and one draw needn't show every extreme that they name: For each image, masked holds 4 * 2**e ones, e drawn evenly from 0 to 6 and the count capped at 256, at positions drawn afresh.
All inputs are finite; a program needn't handle non-finite values.
Results may differ from the reference program's by a relative error of at most 0.024.
Values may be sent and summed in bfloat16 or wider, within the bound.
No kernel may reach another device: no remote copies, remote signals or barrier semaphores. Data moves between devices by JAX's collectives and lax.ppermute only.
A program may use at most 384 MiB of HBM per device.

```python
import math
import jax
import jax.numpy as jnp
from jax import lax

D = 1152
HEADS = 16
HEAD = 72
FF = 4608
DT = 4096
SEQ = 256
TEXT = 32
IMAGES = 64


def shuffled(subkey):
    return jax.random.permutation(subkey, SEQ).astype(jnp.int32)


def draw_masked(key, part):
    key = jax.random.fold_in(key, 7)
    count_key, order_key = jax.random.split(key)
    powers = jax.random.randint(count_key, (IMAGES,), 0, 7).astype(jnp.int32)
    counts = jnp.minimum(jnp.left_shift(jnp.full((IMAGES,), 4, jnp.int32), powers), SEQ)
    orders = jax.vmap(shuffled)(jax.random.split(order_key, IMAGES))
    return (orders < counts[:, None]).astype(jnp.int32)


def steps_of(own_key, shape, cuts, low, largest):
    loudness, own = 1.0, jax.random.fold_in(own_key, 6)
    for position, blocks in cuts:
        draws = jnp.exp(jax.random.uniform(jax.random.fold_in(own, position), (blocks,), jnp.float32, low / len(cuts), largest / len(cuts)))
        loudness = loudness * jnp.repeat(draws, shape[position] // blocks).reshape([-1 if axis == position else 1 for axis in range(len(shape))])
    return loudness


def scatter_about(key, extent, scale, bound, shards=(), dtype=jnp.bfloat16):
    drawn = scale * jax.random.normal(key, extent, jnp.float32)
    if shards:
        drawn = drawn * steps_of(key, extent, shards, -0.22, 0.18)
    return jnp.clip(drawn, -bound, bound).astype(dtype)


def setup_inputs(seed: int = 0) -> dict:
    key_of = jax.random.split(jax.random.key(seed), 17)
    inputs = scatter_about(key_of[0], (IMAGES, SEQ, D), 1.0, 6.0, ((0, 64), (1, 2)))
    text = scatter_about(key_of[1], (IMAGES, TEXT, DT), 1.0, 6.0, ((0, 64), (1, 2)))
    masked = draw_masked(jax.random.fold_in(key_of[16], 71), 0)
    cot = scatter_about(key_of[3], (IMAGES, SEQ, D), 1.0, 6.0, ((0, 64), (1, 2)))
    norm_gains = jnp.clip(1.0 + 0.1 * jax.random.normal(key_of[4], (3, D), jnp.float32), 0.5, 1.5).astype(jnp.bfloat16)
    norm_biases = scatter_about(key_of[5], (3, D), 0.3, 2.0, ((1, 128),))
    w_qkv = scatter_about(key_of[6], (D, 3 * D), D ** -0.5, 0.1875, ((0, 128),))
    w_out = scatter_about(key_of[7], (D, D), (D // 16) ** -0.5, 0.75, ((0, 128),))
    w_text = scatter_about(key_of[8], (DT, D), DT ** -0.5, 0.09375, ((0, 128),))
    w_query = scatter_about(key_of[9], (D, D), D ** -0.5, 0.1875, ((0, 128),))
    w_memory = scatter_about(key_of[10], (D, 2 * D), D ** -0.5, 0.1875, ((0, 128),))
    w_cross_out = scatter_about(key_of[11], (D, D), (D // 4) ** -0.5, 0.375, ((0, 128),))
    w_up = scatter_about(key_of[12], (D, FF), D ** -0.5, 0.1875, ((0, 128),))
    up_bias = scatter_about(key_of[13], (FF,), 0.3, 2.0, ((0, 128),))
    w_down = scatter_about(key_of[14], (FF, D), FF ** -0.5, 0.09375, ((0, 128),))
    down_bias = scatter_about(key_of[15], (D,), 0.3, 2.0, ((0, 128),))
    return dict(inputs=inputs, text=text, masked=masked, cot=cot, norm_gains=norm_gains, norm_biases=norm_biases, w_qkv=w_qkv, w_out=w_out, w_text=w_text, w_query=w_query, w_memory=w_memory, w_cross_out=w_cross_out, w_up=w_up, up_bias=up_bias, w_down=w_down, down_bias=down_bias)


@jax.custom_vjp
def low(v):
    return lax.optimization_barrier(v.astype(jnp.bfloat16)).astype(jnp.float32)

@jax.custom_vjp
def low_back(v):
    return v

def low_keep(v):
    return (low(v), None)

def low_pass(kept, grad):
    return (grad,)

def back_keep(v):
    return (v, None)

def back_low(kept, grad):
    return (low(grad),)
low.defvjp(low_keep, low_pass)
low_back.defvjp(back_keep, back_low)

def product(left, right):
    return jnp.dot(left, right, precision=lax.Precision.HIGHEST)

def normalize(values, gain, shift):
    center = values - lax.optimization_barrier(jnp.mean(values, -1, keepdims=True))
    spread = lax.optimization_barrier(jnp.mean(center * center, -1, keepdims=True))
    return center * lax.rsqrt(spread + 1e-05) * gain + shift

def attention(queries, keys, values):
    count = queries.shape[0]
    length = keys.shape[0]
    query_heads = queries.reshape(count, HEADS, HEAD)
    key_heads = keys.reshape(length, HEADS, HEAD)
    value_heads = values.reshape(length, HEADS, HEAD)
    raw = jnp.einsum('qhd,khd->hqk', query_heads, key_heads, precision=lax.Precision.HIGHEST)
    scores = low_back(raw * HEAD ** (-0.5))
    probs = low(jax.nn.softmax(scores, axis=-1))
    mixed = jnp.einsum('hqk,khd->qhd', probs, value_heads, precision=lax.Precision.HIGHEST)
    return low(low_back(mixed.reshape(count, HEADS * HEAD)))

def image_forward(params, resid, words):
    gains, shifts, w_qkv, w_out, w_text, w_query, w_memory, w_cross_out, w_up, up_bias, w_down, down_bias = params
    joined = low(low_back(product(low(normalize(resid, gains[0], shifts[0])), w_qkv)))
    second = resid + low_back(product(attention(joined[:, :D], joined[:, D:2 * D], joined[:, 2 * D:]), w_out))
    queries = low(low_back(product(low(normalize(second, gains[1], shifts[1])), w_query)))
    projected = low(low_back(product(words, w_text)))
    memory = low(low_back(product(projected, w_memory)))
    third = second + low_back(product(attention(queries, memory[:, :D], memory[:, D:]), w_cross_out))
    upward = low_back(product(low(normalize(third, gains[2], shifts[2])), w_up) + up_bias)
    hidden = low(jax.nn.gelu(upward))
    return third + low_back(product(hidden, w_down) + down_bias)

def reference(inputs, text, masked, cot, norm_gains, norm_biases, w_qkv, w_out, w_text, w_query, w_memory, w_cross_out, w_up, up_bias, w_down, down_bias):
    params = tuple((item.astype(jnp.float32) for item in (norm_gains, norm_biases, w_qkv, w_out, w_text, w_query, w_memory, w_cross_out, w_up, up_bias, w_down, down_bias)))
    group = math.gcd(IMAGES, 16)
    rounds = IMAGES // group

    def regroup(array):
        return array.reshape((rounds, group) + array.shape[1:])
    pulled = cot.astype(jnp.float32) * masked.astype(jnp.float32)[:, :, None]
    batches = (regroup(inputs.astype(jnp.float32)), regroup(text.astype(jnp.float32)), regroup(pulled))

    def forward(weights, resid, words):
        return jax.vmap(image_forward, in_axes=(None, 0, 0))(weights, resid, words)

    def advance(totals, batch):
        resid, words, upstream = batch
        result, pull = jax.vjp(lambda weights, start: forward(weights, start, words), params, resid)
        weight_grads, input_grad = pull(upstream)
        totals = jax.tree.map(jnp.add, totals, weight_grads)
        return (totals, (result.astype(jnp.bfloat16), input_grad))
    zeros = jax.tree.map(jnp.zeros_like, params)
    totals, (outputs, input_grads) = lax.scan(advance, zeros, batches)
    return (outputs.reshape(IMAGES, SEQ, D), input_grads.reshape(IMAGES, SEQ, D), totals[0], totals[1], totals[2], totals[3], totals[4], totals[5], totals[6], totals[7], totals[8], totals[9], totals[10], totals[11])
```

```python
import jax
import jax.numpy as jnp
from jax import lax
from jax.sharding import Mesh, PartitionSpec as P

HEAD = 72
BF = jnp.bfloat16
F32 = jnp.float32
AXES = ("z", "x", "v", "c", "u")
DP = ("z", "x", "v", "c")
NAMES = {"z": ("z", "c"), "x": ("x", "c"), "y": ("v", "c", "u")}


def normalize(values, gain, shift):
    center = values - jnp.mean(values, -1, keepdims=True)
    spread = jnp.mean(center * center, -1, keepdims=True)
    return center * lax.rsqrt(spread + 1e-05) * gain + shift


def norm_back(values, gain, shift, upstream):
    result, pull = jax.vjp(normalize, values, gain, shift)
    return pull(upstream)


def dot(left, right):
    return jnp.dot(left, right, preferred_element_type=F32)


def dot_nt(left, right):
    return lax.dot_general(left, right, (((1,), (1,)), ((), ())), preferred_element_type=F32)


def dot_tn(left, right):
    return lax.dot_general(left, right, (((0,), (0,)), ((), ())), preferred_element_type=F32)


def attend(queries, keys, values, score_scale):
    scores = jnp.einsum("qhd,khd->hqk", queries, keys, preferred_element_type=F32) * score_scale
    highest = jnp.max(scores, -1, keepdims=True)
    log_total = highest + jnp.log(jnp.sum(jnp.exp(scores - highest), -1, keepdims=True))
    probs = jnp.exp(scores - log_total).astype(BF)
    mixed = jnp.einsum("hqk,khd->qhd", probs, values, preferred_element_type=F32)
    return (mixed.astype(BF), log_total)


def attend_back(queries, keys, values, log_total, upstream, score_scale):
    scores = jnp.einsum("qhd,khd->hqk", queries, keys, preferred_element_type=F32) * score_scale
    probs = jnp.exp(scores - log_total)
    probs_grad = jnp.einsum("qhd,khd->hqk", upstream, values, preferred_element_type=F32)
    value_grad = jnp.einsum("hqk,qhd->khd", probs.astype(BF), upstream, preferred_element_type=F32)
    scores_grad = (probs * (probs_grad - jnp.sum(probs * probs_grad, -1, keepdims=True))).astype(BF)
    query_grad = (
        jnp.einsum("hqk,khd->qhd", scores_grad, keys, preferred_element_type=F32) * score_scale
    ).astype(BF)
    key_grad = jnp.einsum("hqk,qhd->khd", scores_grad, queries, preferred_element_type=F32) * score_scale
    return (query_grad, key_grad, value_grad)


def swap(value):
    return lax.ppermute(value, "c", [(0, 1), (1, 0)])


def position_index(axis, place, core):
    if axis == "y":
        return ((place % 2) * 2 + core) * 2 + place // 2
    return place * 2 + core


def receive(value, axis, step, mirrored=True):
    pairs = []
    for core in range(2):
        own = -step if mirrored and core == 1 else step
        for place in range(4):
            pairs.append(
                (position_index(axis, (place + own) % 4, core), position_index(axis, place, core))
            )
    return lax.ppermute(value, NAMES[axis], pairs)


def place_of(axis):
    if axis == "y":
        return 2 * lax.axis_index("u") + lax.axis_index("v")
    return lax.axis_index(axis)


def sign_of():
    return 1 - 2 * lax.axis_index("c")


def places(axis):
    here, sign = place_of(axis), sign_of()
    mine = [here, (here + sign) % 4, (here - sign) % 4, (here + 2) % 4]
    return mine, [mine[0], mine[2], mine[1], mine[3]]


def by_place(pieces, spots):
    slots = jnp.arange(4).reshape((4,) + (1,) * pieces[0].ndim)
    out = pieces[3][None]
    for piece, spot in zip(pieces[:3], spots[:3]):
        out = jnp.where(slots == spot, piece[None], out)
    return out


def gather_small(value, axis):
    pieces = [
        value,
        receive(value, axis, 1),
        receive(value, axis, -1),
        receive(value, axis, 2, False),
    ]
    return by_place(pieces, places(axis)[0])


def gather_large(value, axis):
    half = value.shape[0] // 2
    first = receive(value, axis, 1)
    second = receive(value, axis, -1)
    far = jnp.concatenate(
        [receive(first[:half], axis, 1), receive(second[half:], axis, -1)], 0
    )
    return [value, first, second, far]


def scatter(pieces, axis):
    own, first, second, far = pieces
    total = own.astype(F32)
    total = total + receive(first.astype(BF), axis, -1).astype(F32)
    total = total + receive(second.astype(BF), axis, 1).astype(F32)
    return total + receive(far.astype(BF), axis, 2, False).astype(F32)


def take(blocks, spot):
    return lax.dynamic_index_in_dim(blocks, spot, 0, keepdims=False)


def scatter_blocks(blocks, axis):
    return scatter([take(blocks, spot) for spot in places(axis)[0]], axis)


class Group:
    def __init__(self, value, axis):
        self.axis = axis
        self.own = gather_large(value, axis)
        self.other = [swap(piece) for piece in self.own]
        self.own_spots, self.other_spots = places(axis)

    def times(self, blocks, other, columns=slice(None)):
        pieces, spots = (self.other, self.other_spots) if other else (self.own, self.own_spots)
        total = 0.0
        for piece, spot in zip(pieces, spots):
            total = total + dot(take(blocks, spot), piece[:, columns])
        return total

    def times_rows(self, blocks, other, rows):
        pieces, spots = (self.other, self.other_spots) if other else (self.own, self.own_spots)
        total = 0.0
        for piece, spot in zip(pieces, spots):
            total = total + dot(take(blocks, spot), piece[rows])
        return total

    def back(self, own, other, columns=slice(None)):
        out = []
        for index, mate in enumerate((0, 2, 1, 3)):
            out.append(
                dot_nt(own, self.own[index][:, columns]) + dot_nt(other, self.other[mate][:, columns])
            )
        return by_place(out, self.own_spots)

    def back_rows(self, value, other, rows):
        pieces, spots = (self.other, self.other_spots) if other else (self.own, self.own_spots)
        return by_place([dot_nt(value, piece[rows]) for piece in pieces], spots)


def pair(left_zero, right_zero, left_one, right_one):
    zero = lax.axis_index("c") == 0
    lefts = jnp.where(zero, left_zero, left_one)
    rights = jnp.where(zero, right_zero, right_one)
    left_out = jnp.where(zero, left_one, left_zero)
    right_out = jnp.where(zero, right_one, right_zero)
    return (
        jnp.concatenate([lefts, swap(left_out)], -2),
        jnp.concatenate([rights, swap(right_out)], -2),
    )


def gradient_pieces(lefts, rights, axis):
    return [dot_tn(take(lefts, spot), rights) for spot in places(axis)[0]]


def per_device(
    inputs,
    text,
    masked,
    cot,
    norm_gains,
    norm_biases,
    w_qkv,
    w_out,
    w_text,
    w_query,
    w_memory,
    w_cross_out,
    w_up,
    up_bias,
    w_down,
    down_bias,
):
    inputs, text, masked, cot = inputs[0], text[0], masked[0], cot[0]
    tokens, width = inputs.shape
    heads = width // HEAD
    wide = w_up.shape[1]
    rows = w_qkv.shape[0]
    scale = HEAD ** (-0.5)
    core = lax.axis_index("c")
    zero = core == 0

    up_sorted = w_up.reshape(rows, 4, 4, 2, 2, 2, 36).transpose(0, 4, 5, 3, 2, 1, 6).reshape(rows, 2, wide // 2)
    half_zero = jnp.concatenate([w_qkv[:, : 2 * width], up_sorted[:, 0], w_out, w_cross_out], 1)
    half_one = jnp.concatenate([w_qkv[:, 2 * width :], w_query, up_sorted[:, 1], w_memory], 1)
    kept = jnp.where(zero, half_zero, half_one)
    came = swap(jnp.where(zero, half_one, half_zero))
    chip = jnp.where(
        jnp.arange(2)[:, None, None] == core, kept[None], came[None]
    ).reshape(2 * rows, -1)
    column = gather_small(chip, "y")
    eight = (
        column.reshape(2, 2, 2, rows, -1).transpose(1, 2, 0, 3, 4).reshape(8 * rows, -1)
    )
    text_down = jnp.concatenate([w_text, w_down], 0)
    text_down = gather_small(text_down, "z")
    text_rows, down_rows = w_text.shape[0], w_down.shape[0]
    text_down = jnp.concatenate(
        [
            text_down[:, :text_rows].reshape(4 * text_rows, width),
            text_down[:, text_rows:].reshape(4 * down_rows, width),
        ],
        0,
    )
    split = 4 * width
    plane = gather_small(eight[:, :split], "x").reshape(32 * rows, split)
    plane_x = gather_small(eight[:, split:], "z").reshape(32 * rows, 2 * width)
    text_down = gather_small(text_down, "x")
    text_down = jnp.concatenate(
        [
            text_down[:, : 4 * text_rows].reshape(16 * text_rows, width),
            text_down[:, 4 * text_rows :].reshape(16 * down_rows, width),
        ],
        0,
    )
    joined_set = Group(plane[:, : 2 * width], "z")
    mixed_set = Group(plane_x, "x")
    low_set = Group(text_down, "y")
    up_set = Group(plane[:, 2 * width :], "z")
    text_part = slice(0, 16 * text_rows)
    down_part = slice(16 * text_rows, None)

    small = jnp.concatenate(
        [norm_gains.reshape(-1), norm_biases.reshape(-1), up_bias, down_bias]
    )
    small = lax.all_to_all(
        jnp.broadcast_to(small, (128, small.shape[0])), AXES, 0, 0, tiled=True
    ).astype(F32)
    gains = small[:, : 3 * rows].reshape(128, 3, rows).transpose(1, 0, 2).reshape(3, width)
    shifts = (
        small[:, 3 * rows : 6 * rows].reshape(128, 3, rows).transpose(1, 0, 2).reshape(3, width)
    )
    up_shift = (
        small[:, 6 * rows : 6 * rows + 36]
        .reshape(4, 4, 2, 2, 2, 36)
        .transpose(3, 4, 2, 1, 0, 5)
        .reshape(2, wide // 2)
    )
    up_shift_own = jnp.where(zero, up_shift[0], up_shift[1])
    up_shift_other = jnp.where(zero, up_shift[1], up_shift[0])
    down_shift = small[:, 6 * rows + 36 :].reshape(width)

    def blocks_z(values):
        return values.reshape(values.shape[0], 4, width // 4).transpose(1, 0, 2)

    def unblock_z(blocks):
        return blocks.transpose(1, 0, 2).reshape(blocks.shape[1], width)

    def blocks_x(values):
        return (
            values.reshape(values.shape[0], 4, 4, HEAD)
            .transpose(2, 0, 1, 3)
            .reshape(4, values.shape[0], width // 4)
        )

    def unblock_x(blocks):
        count = blocks.shape[1]
        return blocks.reshape(4, count, 4, HEAD).transpose(1, 2, 0, 3).reshape(count, width)

    def blocks_y(values):
        return values.reshape(values.shape[0], 4, values.shape[1] // 4).transpose(1, 0, 2)

    def unblock_y(blocks):
        return blocks.transpose(1, 0, 2).reshape(blocks.shape[1], 4 * blocks.shape[2])

    def heads_of(values):
        return values.reshape(values.shape[0], heads, HEAD)

    def flat(values):
        return values.reshape(values.shape[0], width)

    def other_half(values):
        return lax.ppermute(values, "u", [(0, 1), (1, 0)])

    words = jnp.concatenate([text, other_half(text)], 0)
    word_blocks = (
        words.reshape(words.shape[0], 4, 4, 2, 2, 2, text_rows)
        .transpose(4, 5, 3, 0, 2, 1, 6)
        .reshape(2, 4, words.shape[0], 16 * text_rows)
    )
    words_own = jnp.where(zero, word_blocks[0], word_blocks[1])
    words_other = jnp.where(zero, word_blocks[1], word_blocks[0])

    resid = inputs.astype(F32)
    first = normalize(resid, gains[0], shifts[0]).astype(BF)
    first_blocks = blocks_z(first)
    own = joined_set.times(first_blocks, False).astype(BF)
    other = joined_set.times(first_blocks, True).astype(BF)
    query_key = jnp.where(zero, own, other)
    values_local = jnp.where(zero, other, own)[:, :width]
    queries = heads_of(query_key[:, :width])
    key_value = jnp.concatenate([query_key[:, width:], values_local], 1)
    key_value = jnp.concatenate([key_value, other_half(key_value)], 0)
    keys = heads_of(key_value[:, :width])
    values = heads_of(key_value[:, width:])
    attended, self_total = attend(queries, keys, values, scale)
    attended = flat(attended)
    attended_blocks = blocks_x(attended)

    def mixed(blocks, columns):
        return (
            mixed_set.times(blocks, False, columns),
            mixed_set.times(blocks, True, columns),
        )

    mine, theirs = mixed(attended_blocks, slice(0, width))
    second = resid + jnp.where(zero, mine, theirs)
    second_in = normalize(second, gains[1], shifts[1]).astype(BF)
    second_blocks = blocks_z(second_in)
    cross_columns = slice(width, 2 * width)
    cross_queries = jnp.where(
        zero,
        joined_set.times(second_blocks, True, cross_columns),
        joined_set.times(second_blocks, False, cross_columns),
    ).astype(BF)
    projected = (
        low_set.times_rows(words_own, False, text_part)
        + low_set.times_rows(words_other, True, text_part)
    ).astype(BF)
    projected_blocks = blocks_x(projected)
    mine, theirs = mixed(projected_blocks, slice(None))
    memory = jnp.where(zero, theirs, mine).astype(BF)
    cross_keys = heads_of(memory[:, :width])
    cross_values = heads_of(memory[:, width:])
    cross_heads = heads_of(cross_queries)
    cross_out, cross_total = attend(cross_heads, cross_keys, cross_values, scale)
    cross_out = flat(cross_out)
    cross_blocks = blocks_x(cross_out)
    mine, theirs = mixed(cross_blocks, cross_columns)
    third = second + jnp.where(zero, mine, theirs)
    third_in = normalize(third, gains[2], shifts[2]).astype(BF)
    third_blocks = blocks_z(third_in)
    upward_own = up_set.times(third_blocks, False) + up_shift_own
    upward_other = up_set.times(third_blocks, True) + up_shift_other
    hidden_own = jax.nn.gelu(upward_own).astype(BF)
    hidden_other = jax.nn.gelu(upward_other).astype(BF)
    hidden_own_blocks = blocks_y(hidden_own)
    hidden_other_blocks = blocks_y(hidden_other)
    final = (
        third
        + low_set.times_rows(hidden_own_blocks, False, down_part)
        + low_set.times_rows(hidden_other_blocks, True, down_part)
        + down_shift
    )
    block_output = final.astype(BF)

    pulled = cot.astype(F32) * masked.astype(F32)[:, None]
    branch = pulled.astype(BF)
    down_shift_grad = jnp.sum(branch.astype(F32), 0)
    hidden_both = jnp.concatenate([hidden_own_blocks, swap(hidden_other_blocks)], 1)
    branch_both = jnp.concatenate([branch, swap(branch)], 0)
    down_pieces = gradient_pieces(hidden_both, branch_both, "y")

    hidden_grad_own = unblock_y(low_set.back_rows(branch, False, down_part))
    hidden_grad_other = unblock_y(low_set.back_rows(branch, True, down_part))
    upward_grad_own = jax.vjp(jax.nn.gelu, upward_own)[1](hidden_grad_own)[0].astype(BF)
    upward_grad_other = jax.vjp(jax.nn.gelu, upward_other)[1](hidden_grad_other)[0].astype(BF)
    up_shift_grad_own = jnp.sum(upward_grad_own.astype(F32), 0)
    up_shift_grad_other = jnp.sum(upward_grad_other.astype(F32), 0)
    third_both = jnp.concatenate([third_blocks, swap(third_blocks)], 1)
    upward_grad_both = jnp.concatenate([upward_grad_own, swap(upward_grad_other)], 0)
    up_pieces = gradient_pieces(third_both, upward_grad_both, "z")
    third_in_grad = unblock_z(up_set.back(upward_grad_own, upward_grad_other))
    third_norm_grad, gain_two, shift_two = norm_back(third, gains[2], shifts[2], third_in_grad)
    third_grad = pulled + third_norm_grad
    cross_branch = third_grad.astype(BF)

    def mixed_back(value, columns):
        return unblock_x(
            by_place(
                [
                    jnp.where(
                        zero,
                        dot_nt(value, mixed_set.own[index][:, columns]),
                        dot_nt(value, mixed_set.other[mate][:, columns]),
                    )
                    for index, mate in enumerate((0, 2, 1, 3))
                ],
                mixed_set.own_spots,
            )
        )

    cross_out_grad = heads_of(mixed_back(cross_branch, cross_columns).astype(BF))
    cross_query_grad, cross_key_grad, cross_value_grad = attend_back(
        cross_heads, cross_keys, cross_values, cross_total, cross_out_grad, scale
    )
    memory_terms = jnp.concatenate([flat(cross_key_grad), flat(cross_value_grad)], 1).astype(BF)
    half_words = text.shape[0]
    memory_grad = (
        memory_terms[:half_words].astype(F32) + other_half(memory_terms[half_words:]).astype(F32)
    ).astype(BF)
    projected_grad = unblock_x(
        by_place(
            [
                jnp.where(
                    zero,
                    dot_nt(memory_grad, mixed_set.other[mate]),
                    dot_nt(memory_grad, mixed_set.own[index]),
                )
                for index, mate in enumerate((0, 2, 1, 3))
            ],
            mixed_set.own_spots,
        )
    ).astype(BF)
    query_flat = flat(cross_query_grad)
    second_in_grad = unblock_z(
        by_place(
            [
                jnp.where(
                    zero,
                    dot_nt(query_flat, joined_set.other[mate][:, cross_columns]),
                    dot_nt(query_flat, joined_set.own[index][:, cross_columns]),
                )
                for index, mate in enumerate((0, 2, 1, 3))
            ],
            joined_set.own_spots,
        )
    )
    second_norm_grad, gain_one, shift_one = norm_back(second, gains[1], shifts[1], second_in_grad)
    second_grad = third_grad + second_norm_grad
    self_branch = second_grad.astype(BF)
    attended_grad = heads_of(mixed_back(self_branch, slice(0, width)).astype(BF))
    query_grad, key_grad, value_grad = attend_back(
        queries, keys, values, self_total, attended_grad, scale
    )
    key_value_grad = jnp.concatenate([flat(key_grad), flat(value_grad)], 1).astype(BF)
    key_value_grad = (
        key_value_grad[:tokens].astype(F32) + other_half(key_value_grad[tokens:]).astype(F32)
    ).astype(BF)
    query_key_grad = jnp.concatenate([flat(query_grad), key_value_grad[:, :width]], 1)
    value_only = key_value_grad[:, width:]
    blank = jnp.zeros_like(value_only)
    value_blank = jnp.concatenate([value_only, blank], 1)
    first_grad = unblock_z(
        joined_set.back(
            jnp.where(zero, query_key_grad, value_blank),
            jnp.where(zero, value_blank, query_key_grad),
        )
    )
    input_norm_grad, gain_zero, shift_zero = norm_back(resid, gains[0], shifts[0], first_grad)
    input_grads = second_grad + input_norm_grad

    query_lefts, query_rights = pair(first_blocks, query_key_grad[:, :width], first_blocks, value_only)
    key_lefts, key_rights = pair(first_blocks, query_key_grad[:, width:], second_blocks, query_flat)
    joined_pieces = [
        jnp.concatenate([one, two], 1)
        for one, two in zip(
            gradient_pieces(query_lefts, query_rights, "z"),
            gradient_pieces(key_lefts, key_rights, "z"),
        )
    ]

    def padded(values):
        return jnp.concatenate(
            [values, jnp.zeros(values.shape[:-2] + (tokens - values.shape[-2], values.shape[-1]), BF)], -2
        )

    word_feature = padded(projected_blocks[:, :half_words])
    out_lefts, out_rights = pair(
        attended_blocks, self_branch, word_feature, padded(memory_grad[:, :width])
    )
    cross_lefts, cross_rights = pair(
        cross_blocks, cross_branch, word_feature, padded(memory_grad[:, width:])
    )
    mixed_pieces = [
        jnp.concatenate([one, two], 1)
        for one, two in zip(
            gradient_pieces(out_lefts, out_rights, "x"),
            gradient_pieces(cross_lefts, cross_rights, "x"),
        )
    ]
    text_lefts = jnp.concatenate(
        [words_own[:, :half_words], swap(words_other[:, :half_words])], 1
    )
    text_rights = jnp.concatenate([projected_grad, swap(projected_grad)], 0)
    text_pieces = gradient_pieces(text_lefts, text_rights, "y")

    def low_finish(pieces, count):
        part = scatter(pieces, "y")
        part = scatter_blocks(part.reshape(4, 4 * count, width), "x")
        return scatter_blocks(part.reshape(4, count, width), "z")

    down_total = low_finish(down_pieces, down_rows)
    text_total = low_finish(text_pieces, text_rows)

    def row_finish(part, axis):
        part = scatter_blocks(part.reshape(4, 8 * rows, -1), axis)
        part = (
            part.reshape(2, 2, 2, rows, -1).transpose(2, 0, 1, 3, 4).reshape(4, 2 * rows, -1)
        )
        part = scatter_blocks(part, "y").reshape(2, rows, -1)
        kept = jnp.where(zero, part[0], part[1])
        came = swap(jnp.where(zero, part[1], part[0]))
        return jnp.where(zero, kept, came), jnp.where(zero, came, kept)

    up_zero, up_one = row_finish(scatter(up_pieces, "z"), "x")
    up_total = (
        jnp.stack([up_zero, up_one], 1)
        .reshape(rows, 2, 2, 2, 4, 4, 36)
        .transpose(0, 5, 4, 3, 1, 2, 6)
        .reshape(rows, wide)
    )
    mixed_zero, mixed_one = row_finish(scatter(mixed_pieces, "x"), "z")
    out_total, cross_total_grad = mixed_zero[:, :width], mixed_zero[:, width:]
    memory_total = mixed_one
    joined_zero, joined_one = row_finish(scatter(joined_pieces, "z"), "x")
    joined_total = jnp.concatenate([joined_zero, joined_one[:, :width]], 1)
    query_total = joined_one[:, width:]

    up_shift_grad = (
        jnp.stack(
            [
                jnp.where(zero, up_shift_grad_own, up_shift_grad_other),
                jnp.where(zero, up_shift_grad_other, up_shift_grad_own),
            ]
        )
        .reshape(2, 2, 2, 4, 4, 36)
        .transpose(4, 3, 2, 0, 1, 5)
        .reshape(128, 36)
    )
    gain_terms = jnp.stack([gain_zero, gain_one, gain_two])
    shift_terms = jnp.stack([shift_zero, shift_one, shift_two])
    small_grads = jnp.concatenate(
        [
            gain_terms.reshape(3, 128, rows).transpose(1, 0, 2).reshape(128, 3 * rows),
            shift_terms.reshape(3, 128, rows).transpose(1, 0, 2).reshape(128, 3 * rows),
            up_shift_grad,
            down_shift_grad.reshape(128, rows),
        ],
        1,
    )
    small_total = jnp.sum(lax.all_to_all(small_grads, AXES, 0, 0, tiled=True), 0)
    gain_total = small_total[: 3 * rows].reshape(3, rows)
    shift_total = small_total[3 * rows : 6 * rows].reshape(3, rows)
    up_shift_total = small_total[6 * rows : 6 * rows + 36]
    down_shift_total = small_total[6 * rows + 36 :]
    return (
        block_output[None],
        input_grads[None],
        gain_total,
        shift_total,
        joined_total,
        out_total,
        text_total,
        query_total,
        memory_total,
        cross_total_grad,
        up_total,
        up_shift_total,
        down_total,
        down_shift_total,
    )


def solution(mesh):
    fine = Mesh(mesh.devices.reshape(4, 4, 2, 2, 2), AXES)
    tokens = P(DP, "u", None)
    split_rows = P(AXES, None)
    split_columns = P(None, AXES)
    split_vector = P(AXES)
    return jax.shard_map(
        per_device,
        mesh=fine,
        in_specs=(tokens, tokens, P(DP, "u"), tokens)
        + (split_columns,) * 2
        + (split_rows,) * 7
        + (split_vector, split_rows, split_vector),
        out_specs=(tokens, tokens)
        + (split_columns,) * 2
        + (split_rows,) * 7
        + (split_vector, split_rows, split_vector),
        check_vma=False,
    )
```

```python
import functools

import jax
import jax.numpy as jnp
from jax import lax
from jax.experimental import pallas as pl
from jax.experimental.pallas import tpu as pltpu
from jax.sharding import Mesh, PartitionSpec as P

HEAD = 72
HEADS = 16
BF = jnp.bfloat16
F32 = jnp.float32
AXES = ("z", "x", "v", "c", "u")
DP = ("z", "x", "v", "c")
NAMES = {"z": ("z", "c"), "x": ("x", "c"), "y": ("v", "c", "u")}


WIDE = 640


def dot(left, right):
    return jnp.dot(left, right, preferred_element_type=F32)


def dot_nt(left, right):
    return lax.dot_general(left, right, (((1,), (1,)), ((), ())), preferred_element_type=F32)


def dot_tn(left, right):
    return lax.dot_general(left, right, (((0,), (0,)), ((), ())), preferred_element_type=F32)


def lane_window(head):
    start = head * HEAD
    low = min(start // 128, (HEADS * HEAD) // 128 - 2) * 128
    return slice(low, low + 256), start - low


def head_mask(offset, rows):
    lane = lax.broadcasted_iota(jnp.int32, (rows, 256), 1)
    return (lane >= offset) & (lane < offset + HEAD)


def only(mask, values):
    return jnp.where(mask, values, jnp.zeros_like(values))


def softmax(scores):
    weights = jnp.exp(scores - jnp.max(scores, -1, keepdims=True))
    return weights * (1.0 / jnp.sum(weights, -1, keepdims=True))


def attend_into(total, query_ref, memory_ref, scale):
    tokens, width = query_ref.shape
    total[...] = jnp.zeros_like(total)
    for head in range(HEADS):
        window, offset = lane_window(head)
        beside = slice(window.start + width, window.stop + width)
        mask = head_mask(offset, tokens)
        scores = dot_nt(only(mask, query_ref[:, window]), memory_ref[:, window]) * scale
        mixed = dot(softmax(scores).astype(BF), memory_ref[:, beside])
        total[:, window] += only(mask, mixed)


def attend_back_into(query_total, memory_total, query_ref, memory_ref, upstream_ref, scale):
    tokens, width = query_ref.shape
    query_total[...] = jnp.zeros_like(query_total)
    memory_total[...] = jnp.zeros_like(memory_total)
    for head in range(HEADS):
        window, offset = lane_window(head)
        beside = slice(window.start + width, window.stop + width)
        mask = head_mask(offset, tokens)
        query = only(mask, query_ref[:, window])
        upstream = only(mask, upstream_ref[:, window])
        probs = softmax(dot_nt(query, memory_ref[:, window]) * scale)
        probs_grad = dot_nt(upstream, memory_ref[:, beside])
        memory_total[:, beside] += dot_tn(probs.astype(BF), upstream)
        scores_grad = (
            probs * (probs_grad - jnp.sum(probs * probs_grad, -1, keepdims=True))
        ).astype(BF)
        query_total[:, window] += only(mask, dot(scores_grad, memory_ref[:, window])) * scale
        memory_total[:, window] += dot_tn(scores_grad, query) * scale


def norm_parts(values):
    center = values - jnp.mean(values, -1, keepdims=True)
    inverse = lax.rsqrt(jnp.mean(center * center, -1, keepdims=True) + 1e-05)
    return center * inverse, inverse


def norm_back(values, gain, upstream):
    hat, inverse = norm_parts(values)
    scaled = upstream * gain
    result = inverse * (
        scaled
        - jnp.mean(scaled, -1, keepdims=True)
        - hat * jnp.mean(scaled * hat, -1, keepdims=True)
    )
    return (
        result,
        jnp.sum(upstream * hat, 0, keepdims=True),
        jnp.sum(upstream, 0, keepdims=True),
    )


def fetch(core_ref, when_zero, when_one, target, sem, columns=None):
    def view(ref):
        return ref if columns is None else ref.at[:, columns]

    zero = core_ref[0] == 0

    @pl.when(zero)
    def _():
        pltpu.make_async_copy(view(when_zero), target, sem).start()

    @pl.when(jnp.logical_not(zero))
    def _():
        pltpu.make_async_copy(view(when_one), target, sem).start()

    return pltpu.make_async_copy(view(when_zero), target, sem).wait


def project_kernel(inputs, norms, own, first, mine, theirs, handed, weight, sems):
    tokens = mine.shape[0]
    copy = pltpu.make_async_copy(own.at[:, : weight.shape[1]], weight, sems.at[0])
    copy.start()
    hat, _ = norm_parts(inputs[...].astype(F32))
    first[...] = (hat * norms[0:1] + norms[1:2]).astype(BF)
    copy.wait()
    mine[...] = dot(first[:tokens], weight[...]).astype(BF)
    theirs[...] = dot(first[tokens:], weight[...]).astype(BF)


def attend_kernel(scale, queries, key_values, attended, total):
    attend_into(total, queries, key_values, scale)
    attended[...] = total[...].astype(BF)


def column_block(index, width):
    start = index * width + (128 if index > 1 else 0)
    return slice(start, start + width)


def forward_kernel(
    scale, core, attended, inputs, words, norms, own, other,
    second, second_in, cross_queries, cross_out, third, third_in,
    out, cross, ask, total, sems,
):
    width = inputs.shape[1]
    wait_out = fetch(core, own, other, out, sems.at[0], column_block(2, width))
    wait_ask = fetch(core, other, own, ask, sems.at[1], column_block(1, width))
    wait_cross = fetch(core, own, other, cross, sems.at[2], column_block(3, width))
    wait_out()
    value = inputs[...].astype(F32) + dot(attended[...], out[...])
    second[...] = value
    hat, _ = norm_parts(value)
    second_in[...] = (hat * norms[2:3] + norms[3:4]).astype(BF)
    wait_ask()
    cross_queries[...] = dot(second_in[...], ask[...]).astype(BF)
    attend_into(total, cross_queries, words, scale)
    cross_out[...] = total[...].astype(BF)
    wait_cross()
    value = second[...] + dot(cross_out[...], cross[...])
    third[...] = value
    hat, _ = norm_parts(value)
    third_in[...] = (hat * norms[4:5] + norms[5:6]).astype(BF)


def cross_back_kernel(
    scale, core, upstream, third, second, cot, masked, words, cross_queries, norms, own, other,
    cross_branch, cross_query_grad, words_grad, self_branch, second_grad, attended_grad, small,
    out, cross, ask, grad, query_total, words_total, sems,
):
    width = third.shape[1]
    wait_cross = fetch(core, own, other, cross, sems.at[2], column_block(3, width))
    wait_ask = fetch(core, other, own, ask, sems.at[1], column_block(1, width))
    wait_out = fetch(core, own, other, out, sems.at[0], column_block(2, width))
    change, gain, shift = norm_back(third[...], norms[4:5], upstream[...])
    small[...] = jnp.zeros_like(small)
    small[2:3] = gain
    small[5:6] = shift
    value = cot[...].astype(F32) * masked[...] + change
    second_grad[...] = value
    cross_branch[...] = value.astype(BF)
    wait_cross()
    grad[...] = dot_nt(cross_branch[...], cross[...]).astype(BF)
    attend_back_into(query_total, words_total, cross_queries, words, grad, scale)
    cross_query_grad[...] = query_total[...].astype(BF)
    words_grad[...] = words_total[...].astype(BF)
    wait_ask()
    change, gain, shift = norm_back(
        second[...], norms[2:3], dot_nt(cross_query_grad[...], ask[...])
    )
    small[1:2] = gain
    small[4:5] = shift
    value = second_grad[...] + change
    second_grad[...] = value
    self_branch[...] = value.astype(BF)
    wait_out()
    attended_grad[...] = dot_nt(self_branch[...], out[...]).astype(BF)


def attend_back_kernel(
    scale, queries, key_values, attended_grad, query_grad, key_grad, value_grad, key_value_else,
    query_total, key_value_total,
):
    tokens, width = queries.shape
    attend_back_into(query_total, key_value_total, queries, key_values, attended_grad, scale)
    query_grad[...] = query_total[...].astype(BF)
    key_grad[...] = key_value_total[:tokens, :width].astype(BF)
    value_grad[...] = key_value_total[:tokens, width:].astype(BF)
    key_value_else[...] = key_value_total[tokens:].astype(BF)


def input_kernel(
    core, query_grad, key_grad, value_grad, inputs, second_grad, norms, own, other, input_grad, small, both, side, sems
):
    width = inputs.shape[1]
    wait_both = fetch(core, own, other, both, sems.at[0], slice(0, 2 * width))
    wait_side = fetch(core, other, own, side, sems.at[1], slice(0, width))
    wait_both()
    upstream = dot_nt(query_grad[...], both[:, :width]) + dot_nt(key_grad[...], both[:, width:])
    wait_side()
    upstream = upstream + dot_nt(value_grad[...], side[...])
    change, gain, shift = norm_back(inputs[...].astype(F32), norms[0:1], upstream)
    input_grad[...] = second_grad[...] + change
    small[...] = jnp.zeros_like(small)
    small[0:1] = gain
    small[1:2] = shift


def words_kernel(core, projected, own, other, words, keys, values, sems):
    width = projected.shape[1]
    wait_keys = fetch(core, other, own, keys, sems.at[0], column_block(2, width))
    wait_values = fetch(core, other, own, values, sems.at[1], column_block(3, width))
    wait_keys()
    words[:, :width] = dot(projected[...], keys[...]).astype(BF)
    wait_values()
    words[:, width:] = dot(projected[...], values[...]).astype(BF)


def words_back_kernel(core, words_grad, own, other, projected_grad, keys, values, sems):
    width = projected_grad.shape[1]
    wait_keys = fetch(core, other, own, keys, sems.at[0], column_block(2, width))
    wait_values = fetch(core, other, own, values, sems.at[1], column_block(3, width))
    wait_keys()
    value = dot_nt(words_grad[:, :width], keys[...])
    wait_values()
    projected_grad[...] = (value + dot_nt(words_grad[:, width:], values[...])).astype(BF)


def weight_kernel(lefts, rights, out):
    out[...] = dot_tn(lefts[0], rights[...]).astype(BF)


def unpack_kernel(packed, up, down):
    part, width = down.shape
    up[...] = packed[:, :part]
    values = packed[:, WIDE:].astype(F32)
    block, down_block = width // 16, part // 16
    for index in range(16):
        rows = slice(index * down_block, (index + 1) * down_block)
        start = index * block
        down[rows, :WIDE] = values[start : start + down_block].astype(BF)
        down[rows, width - WIDE :] = values[start + down_block : start + block].astype(BF)


def feed_forward_kernel(third, upward_grad, hidden, branch, out):
    part = hidden.shape[1]
    block, down_block = third.shape[1] // 16, part // 16
    up = dot_tn(third[...], upward_grad[...])
    out[:, :, part : WIDE] = jnp.zeros((16, block, WIDE - part), BF)
    out[:, :, WIDE + part :] = jnp.zeros((16, block, WIDE - part), BF)
    for index in range(16):
        out[index, :, :part] = up[index * block : (index + 1) * block].astype(BF)
    for half in range(2):
        down = dot_tn(hidden[...], branch[:, half * part : (half + 1) * part])
        for index in range(16):
            out[index, half * down_block : (half + 1) * down_block, WIDE : WIDE + part] = down[
                index * down_block : (index + 1) * down_block
            ].astype(BF)


def call(kernel, ins, outs, scratch, earlier=(), moved=1, handed=None):
    spaces = {"v": pltpu.VMEM, "s": pltpu.SMEM, "a": pl.ANY}
    held = jax.tree.leaves(earlier)
    count = len(ins)
    last = [] if handed is None else [handed]
    outs = outs + [(ins[index][0].shape, ins[index][0].dtype) for index in last]

    def body(*refs):
        kernel(*refs[:count], *refs[count + len(held) :])

    return pl.pallas_call(
        body,
        in_specs=[pl.BlockSpec(memory_space=spaces[space]) for _, space in ins]
        + [pl.BlockSpec(memory_space=pl.ANY)] * len(held),
        out_specs=[pl.BlockSpec(memory_space=pltpu.VMEM) for _ in outs[: len(outs) - len(last)]]
        + [pl.BlockSpec(memory_space=pl.ANY)] * len(last),
        out_shape=[jax.ShapeDtypeStruct(shape, dtype) for shape, dtype in outs],
        input_output_aliases={index: len(outs) - 1 for index in last},
        scratch_shapes=scratch,
        cost_estimate=pl.CostEstimate(flops=1, bytes_accessed=moved, transcendentals=0),
        compiler_params=pltpu.CompilerParams(vmem_limit_bytes=56 * 2**20),
    )(*[array for array, _ in ins], *held)


def weight_gradient(lefts, rights, half, base=None, earlier=()):
    parts, tokens, rows = lefts.shape
    columns = rights.shape[1]
    tile = 384
    steps = columns // parts // tile
    held = ([] if base is None else [base]) + jax.tree.leaves(earlier)

    def body(lefts_ref, rights_ref, *refs):
        weight_kernel(lefts_ref, rights_ref, refs[-1])

    return pl.pallas_call(
        body,
        grid=(parts * steps,),
        in_specs=[
            pl.BlockSpec((1, tokens, rows), lambda step: (step // steps, 0, 0)),
            pl.BlockSpec((tokens, tile), lambda step: (0, step)),
        ]
        + [pl.BlockSpec(memory_space=pl.ANY)] * len(held),
        out_specs=pl.BlockSpec((rows, tile), lambda step: (0, step + half * parts * steps)),
        out_shape=jax.ShapeDtypeStruct((rows, 2 * columns), BF),
        input_output_aliases={} if base is None else {2: 0},
        cost_estimate=pl.CostEstimate(flops=1, bytes_accessed=1, transcendentals=0),
        compiler_params=pltpu.CompilerParams(vmem_limit_bytes=56 * 2**20),
    )(lefts, rights, *held)


def after(values, *earlier):
    flat, tree = jax.tree.flatten(values)
    held = jax.tree.leaves(earlier)
    outs = pl.pallas_call(
        lambda *refs: None,
        in_specs=[pl.BlockSpec(memory_space=pl.ANY)] * (len(flat) + len(held)),
        out_specs=[pl.BlockSpec(memory_space=pl.ANY)] * len(flat),
        out_shape=[jax.ShapeDtypeStruct(value.shape, value.dtype) for value in flat],
        input_output_aliases={index: index for index in range(len(flat))},
        cost_estimate=pl.CostEstimate(flops=1, bytes_accessed=1, transcendentals=0),
    )(*flat, *held)
    return jax.tree.unflatten(tree, outs)


def swap(value):
    return lax.ppermute(value, "c", [(0, 1), (1, 0)])


def position_index(axis, place, core):
    if axis == "y":
        return ((place % 2) * 2 + core) * 2 + place // 2
    return place * 2 + core


def receive(value, axis, step, mirrored=True):
    pairs = []
    for core in range(2):
        own = -step if mirrored and core == 1 else step
        for place in range(4):
            pairs.append(
                (position_index(axis, (place + own) % 4, core), position_index(axis, place, core))
            )
    return lax.ppermute(value, NAMES[axis], pairs)


def place_of(axis):
    if axis == "y":
        return 2 * lax.axis_index("u") + lax.axis_index("v")
    return lax.axis_index(axis)


def sign_of():
    return 1 - 2 * lax.axis_index("c")


def places(axis):
    here, sign = place_of(axis), sign_of()
    mine = [here, (here + sign) % 4, (here - sign) % 4, (here + 2) % 4]
    return mine, [mine[0], mine[2], mine[1], mine[3]]


def by_place(pieces, spots):
    slots = jnp.arange(4).reshape((4,) + (1,) * pieces[0].ndim)
    out = pieces[3][None]
    for piece, spot in zip(pieces[:3], spots[:3]):
        out = jnp.where(slots == spot, piece[None], out)
    return out


def gather_direct(value, axis):
    return [
        value,
        receive(value, axis, 1),
        receive(value, axis, -1),
        receive(value, axis, 2, False),
    ]


def scatter(pieces, axis):
    own, first, second, far = pieces
    total = own.astype(F32)
    total = total + receive(first.astype(BF), axis, -1).astype(F32)
    total = total + receive(second.astype(BF), axis, 1).astype(F32)
    return total + receive(far.astype(BF), axis, 2, False).astype(F32)


def take(blocks, spot):
    return lax.dynamic_index_in_dim(blocks, spot, 0, keepdims=False)


def scatter_blocks(blocks, axis):
    return scatter([take(blocks, spot) for spot in places(axis)[0]], axis)


def exchange(blocks, axes):
    return lax.all_to_all(blocks, axes, 0, 0, tiled=True)


def spread(value, axes, count):
    return exchange(jnp.broadcast_to(value[None], (count,) + value.shape), axes)


def exchange_sum(blocks, axes):
    return jnp.sum(exchange(blocks.astype(BF), axes).astype(F32), 0)


def gather_plane(value):
    return lax.all_gather(value, ("z", "x"), axis=0, tiled=True)


def scatter_plane(value, axes=("z", "x")):
    blocks = value.reshape(16, value.shape[0] // 16, value.shape[1])
    return lax.psum_scatter(blocks, axes, scatter_dimension=0, tiled=True)[0]


def pair_one(when_zero, when_one):
    zero = lax.axis_index("c") == 0
    return jnp.concatenate(
        [jnp.where(zero, when_zero, when_one), swap(jnp.where(zero, when_one, when_zero))], -2
    )


def pair(left_zero, right_zero, left_one, right_one):
    return pair_one(left_zero, left_one), pair_one(right_zero, right_one)


def per_device(
    inputs,
    text,
    masked,
    cot,
    norm_gains,
    norm_biases,
    w_qkv,
    w_out,
    w_text,
    w_query,
    w_memory,
    w_cross_out,
    w_up,
    up_bias,
    w_down,
    down_bias,
):
    inputs, text, masked, cot = inputs[0], text[0], masked[0], cot[0]
    tokens, width = inputs.shape
    half_words = text.shape[0]
    wide = w_up.shape[1]
    part = wide // 8
    rows = w_qkv.shape[0]
    text_rows, down_rows = w_text.shape[0], w_down.shape[0]
    scale = HEAD ** (-0.5)
    core = lax.axis_index("c")
    zero = core == 0
    core_word = core.astype(jnp.int32).reshape(1)
    group = ("v", "c", "u")
    inputs_both = jnp.concatenate([inputs, swap(inputs)], 0)

    extra = jnp.concatenate(
        [
            jnp.stack([norm_gains, norm_biases], 1).reshape(6, rows).T,
            up_bias.reshape(rows, -1),
            down_bias[:, None],
        ],
        1,
    )
    extra = jnp.pad(extra, ((0, 0), (0, 128 - extra.shape[1])))
    half_zero = jnp.concatenate([w_qkv[:, : 2 * width], extra, w_out, w_cross_out], 1)
    half_one = jnp.concatenate([w_qkv[:, 2 * width :], w_query, extra, w_memory], 1)
    kept = jnp.where(zero, half_zero, half_one)
    came = swap(jnp.where(zero, half_one, half_zero))
    chip = jnp.where(
        jnp.arange(2)[:, None, None] == core, kept[None], came[None]
    ).reshape(2 * rows, -1)

    own = gather_plane(
        by_place(gather_direct(chip, "y"), places("y")[0])
        .reshape(2, 2, 2, rows, -1)
        .transpose(1, 2, 0, 3, 4)
        .reshape(8 * rows, -1)
    )

    parts = jnp.concatenate(
        [
            w_up.reshape(rows, 16, 8, down_rows).transpose(2, 0, 1, 3).reshape(8, -1),
            text.reshape(half_words, 16, 8, text_rows).transpose(2, 0, 1, 3).reshape(8, -1),
        ],
        1,
    )
    parts = exchange(parts, group)
    text_all = parts[:, rows * part :].reshape(8 * half_words, 16 * text_rows)
    text_weight = spread(w_text, ("z", "x"), 16).reshape(-1, width)

    def other_half(values):
        return lax.ppermute(values, "u", [(0, 1), (1, 0)])

    projected = dot(text_all, text_weight).reshape(2, 2, 2 * half_words, width)
    projected = jnp.where(zero, projected[:, 0], projected[:, 1]) + swap(
        jnp.where(zero, projected[:, 1], projected[:, 0])
    )
    lower = lax.axis_index("v") == 0
    elsewhere = jnp.where(lower, projected[1], projected[0])
    projected = jnp.where(lower, projected[0], projected[1])
    projected = (
        projected
        + receive(elsewhere, "y", 1)
        + receive(elsewhere, "y", -1)
        + receive(projected, "y", 2, False)
    ).astype(BF)

    own = after(own, projected)

    eighth = jnp.concatenate(
        [
            parts[:, : rows * part].reshape(8 * rows, part),
            jnp.zeros((8 * rows, WIDE - part), BF),
            jnp.concatenate([w_down[:, :WIDE], w_down[:, width - WIDE :]], 0),
        ],
        1,
    )
    eighth = gather_plane(eighth)

    shifts = own[:, 2 * width : 2 * width + 128].astype(F32)
    norms = shifts[:, :6].T

    def both_cores(ring):
        ring = jnp.concatenate(ring, 0)
        return jnp.concatenate([ring, swap(ring)], 0)

    def fold_tokens(values):
        ring = values[: 4 * tokens] + swap(values[4 * tokens :].astype(BF)).astype(F32)
        return [ring[index * tokens : (index + 1) * tokens] for index in range(4)]

    first, mine, theirs, own = call(
        project_kernel,
        [(inputs_both, "v"), (norms, "v"), (own, "a")],
        [((2 * tokens, width), BF), ((tokens, 2 * width), BF), ((tokens, 2 * width), BF)],
        [pltpu.VMEM((width, 2 * width), BF), pltpu.SemaphoreType.DMA((1,))],
        handed=2,
    )
    theirs = swap(theirs)
    queries = jnp.where(zero, mine[:, :width], theirs[:, :width])
    key_value = jnp.concatenate(
        [
            jnp.where(zero, mine[:, width:], theirs[:, width:]),
            jnp.where(zero, theirs[:, :width], mine[:, :width]),
        ],
        1,
    )
    other = swap(own)
    key_value = jnp.concatenate([key_value, other_half(key_value)], 0)
    weights = [(own, "a"), (other, "a")]
    words = call(
        words_kernel,
        [(core_word, "s"), (projected, "v")] + weights,
        [((2 * half_words, 2 * width), BF)],
        [
            pltpu.VMEM((width, width), BF),
            pltpu.VMEM((width, width), BF),
            pltpu.SemaphoreType.DMA((2,)),
        ],
    )[0]
    attended = call(
        functools.partial(attend_kernel, scale),
        [(queries, "v"), (key_value, "v")],
        [((tokens, width), BF)],
        [pltpu.VMEM((tokens, width), F32)],
        [words],
    )[0]
    second, second_in, cross_queries, cross_out, third, third_in = call(
        functools.partial(forward_kernel, scale),
        [(core_word, "s"), (attended, "v"), (inputs, "v"), (words, "v"), (norms, "v")]
        + weights,
        [
            ((tokens, width), F32),
            ((tokens, width), BF),
            ((tokens, width), BF),
            ((tokens, width), BF),
            ((tokens, width), F32),
            ((tokens, width), BF),
        ],
        [
            pltpu.VMEM((width, width), BF),
            pltpu.VMEM((width, width), BF),
            pltpu.VMEM((width, width), BF),
            pltpu.VMEM((tokens, width), F32),
            pltpu.SemaphoreType.DMA((3,)),
        ],
    )
    loss_tokens = masked.astype(F32)[:, None]
    branch = (cot.astype(F32) * loss_tokens).astype(BF)
    branch_ring = gather_direct(after(branch, attended), "y")
    down_shift_grad = jnp.sum(branch.astype(F32), 0)
    shifts, branch_ring = after((shifts, branch_ring), third_in)
    branch_all = both_cores(branch_ring)
    place = (lax.axis_index("v") * 2 + core) * 2 + lax.axis_index("u")
    up_shift = lax.dynamic_index_in_dim(
        shifts[:, 6:10].reshape(16, 8, down_rows), place, 1, False
    ).reshape(part)
    down_shift = shifts[:, 10]
    up_weight, down_weight = call(
        unpack_kernel,
        [(eighth, "v")],
        [((width, part), BF), ((part, width), BF)],
        [],
        [third_in],
    )

    third_all = both_cores(gather_direct(third_in, "y"))
    hidden_grad = dot_nt(branch_all, down_weight)
    upward = dot(third_all, up_weight) + up_shift
    upward_grad = jax.vjp(jax.nn.gelu, upward)[1](hidden_grad)[0].astype(BF)
    hidden = jax.nn.gelu(upward).astype(BF)
    third_in_grad = fold_tokens(dot_nt(upward_grad, up_weight))
    up_down_grad = call(
        feed_forward_kernel,
        [(third_all, "v"), (upward_grad, "v"), (hidden, "v"), (branch_all, "v")],
        [((16, 8 * rows, 2 * WIDE), BF)],
        [],
        third_in_grad,
        2**25,
    )[0]
    third_in_grad = scatter(third_in_grad, "y")
    up_down_parts = exchange(up_down_grad, ("z", "x"))
    up_shift_grad = jnp.sum(upward_grad.astype(F32), 0)

    (
        cross_branch,
        cross_query_grad,
        words_grad,
        self_branch,
        second_grad,
        attended_grad,
        norm_grads,
    ) = call(
        functools.partial(cross_back_kernel, scale),
        [
            (core_word, "s"),
            (third_in_grad, "v"),
            (third, "v"),
            (second, "v"),
            (cot, "v"),
            (loss_tokens, "v"),
            (words, "v"),
            (cross_queries, "v"),
            (norms, "v"),
        ]
        + weights,
        [
            ((tokens, width), BF),
            ((tokens, width), BF),
            ((2 * half_words, 2 * width), BF),
            ((tokens, width), BF),
            ((tokens, width), F32),
            ((tokens, width), BF),
            ((8, width), F32),
        ],
        [
            pltpu.VMEM((width, width), BF),
            pltpu.VMEM((width, width), BF),
            pltpu.VMEM((width, width), BF),
            pltpu.VMEM((tokens, width), BF),
            pltpu.VMEM((tokens, width), F32),
            pltpu.VMEM((2 * half_words, 2 * width), F32),
            pltpu.SemaphoreType.DMA((3,)),
        ],
        [up_down_grad],
    )
    query_grad, key_grad, value_grad, key_value_else = call(
        functools.partial(attend_back_kernel, scale),
        [(queries, "v"), (key_value, "v"), (attended_grad, "v")],
        [
            ((tokens, width), BF),
            ((tokens, width), BF),
            ((tokens, width), BF),
            ((tokens, 2 * width), BF),
        ],
        [pltpu.VMEM((tokens, width), F32), pltpu.VMEM((2 * tokens, 2 * width), F32)],
    )
    words_part = words_grad
    words_grad = (words_grad.astype(F32) + other_half(words_grad).astype(F32)).astype(BF)
    projected_grad = call(
        words_back_kernel,
        [(core_word, "s"), (words_grad, "v")] + weights,
        [((2 * half_words, width), BF)],
        [
            pltpu.VMEM((width, width), BF),
            pltpu.VMEM((width, width), BF),
            pltpu.SemaphoreType.DMA((2,)),
        ],
        [key_value_else],
    )[0]

    elsewhere = receive(projected_grad, "y", 1)

    def padded(values):
        return jnp.pad(values, ((0, tokens - values.shape[0]), (0, 0)))

    mixed_lefts, mixed_rights = pair(
        jnp.stack([attended, cross_out]),
        jnp.concatenate([self_branch, cross_branch], 1),
        jnp.stack([padded(projected)] * 2),
        padded(words_part),
    )
    attention_grad = weight_gradient(mixed_lefts, mixed_rights, 1, earlier=[key_value_else])
    theirs = after(other_half(key_value_else), attention_grad, projected_grad)
    key_grad = (key_grad.astype(F32) + theirs[:, :width].astype(F32)).astype(BF)
    value_grad = (value_grad.astype(F32) + theirs[:, width:].astype(F32)).astype(BF)
    joined_rights = pair_one(
        jnp.concatenate([query_grad, key_grad], 1),
        jnp.concatenate([value_grad, cross_query_grad], 1),
    )
    second_both = pair_one(second_in, second_in)
    first_right = jnp.where(zero, first, second_both)
    attention_grad = weight_gradient(
        jnp.stack([first, first_right]), joined_rights, 0, attention_grad, [up_down_parts]
    )

    input_grads, last_grads = call(
        input_kernel,
        [
            (core_word, "s"),
            (query_grad, "v"),
            (key_grad, "v"),
            (value_grad, "v"),
            (inputs, "v"),
            (second_grad, "v"),
            (norms, "v"),
        ]
        + weights,
        [((tokens, width), F32), ((8, width), F32)],
        [
            pltpu.VMEM((width, 2 * width), BF),
            pltpu.VMEM((width, width), BF),
            pltpu.SemaphoreType.DMA((2,)),
        ],
        [attention_grad],
    )
    images = jnp.stack(
        [jnp.where(lower, projected_grad, elsewhere), jnp.where(lower, elsewhere, projected_grad)]
    )
    theirs = swap(images)
    projected_grad = jnp.stack(
        [jnp.where(zero, images, theirs), jnp.where(zero, theirs, images)], 1
    ).reshape(8 * half_words, width)
    text_grad = dot_tn(text_all, projected_grad)

    final = third + scatter(
        fold_tokens(dot(after(hidden, attention_grad), down_weight)), "y"
    ) + down_shift
    block_output = final.astype(BF)

    up_down_total = jnp.sum(up_down_parts.astype(F32), 0)
    down_total = jnp.concatenate(
        [
            up_down_total[:down_rows, WIDE : WIDE + part],
            up_down_total[down_rows:, WIDE : WIDE + part],
        ],
        1,
    )
    up_total = (
        lax.all_to_all(up_down_total[:, :part].reshape(8, rows, part), group, 0, 0, tiled=True)
        .reshape(8, rows, 16, down_rows)
        .transpose(1, 2, 0, 3)
        .reshape(rows, wide)
    )

    text_total = exchange_sum(
        after(text_grad.reshape(16, text_rows, width), up_total), ("z", "x")
    )

    by_place_part = jnp.where(
        jnp.arange(8)[None, :, None] == place, up_shift_grad.reshape(16, 1, down_rows), 0.0
    ).reshape(128, down_rows)
    gain_terms = jnp.concatenate([last_grads[:1], norm_grads[1:3]], 0)
    shift_terms = jnp.concatenate([last_grads[1:2], norm_grads[4:6]], 0)
    small_grads = jnp.concatenate(
        [
            gain_terms.reshape(3, 128, rows).transpose(1, 0, 2).reshape(128, 3 * rows),
            shift_terms.reshape(3, 128, rows).transpose(1, 0, 2).reshape(128, 3 * rows),
            by_place_part,
            down_shift_grad.reshape(128, rows),
        ],
        1,
    )
    small_total = jnp.sum(exchange(after(small_grads, text_total), AXES), 0)
    gain_total = small_total[: 3 * rows].reshape(3, rows)
    shift_total = small_total[3 * rows : 6 * rows].reshape(3, rows)
    up_shift_total = small_total[6 * rows : 6 * rows + down_rows]
    down_shift_total = small_total[6 * rows + down_rows :]

    total = scatter_plane(attention_grad).reshape(8, rows, -1)
    total = exchange(after(total, small_total), group).astype(F32)
    total_zero, total_one = jnp.sum(total.reshape(2, 2, 2, rows, -1), (0, 2))
    joined_total = jnp.concatenate([total_zero[:, : 2 * width], total_one[:, :width]], 1)
    query_total = total_one[:, width : 2 * width]
    out_total = total_zero[:, 2 * width : 3 * width]
    cross_total_grad = total_zero[:, 3 * width :]
    memory_total = total_one[:, 2 * width :]
    return (
        block_output[None],
        input_grads[None],
        gain_total,
        shift_total,
        joined_total,
        out_total,
        text_total,
        query_total,
        memory_total,
        cross_total_grad,
        up_total,
        up_shift_total,
        down_total,
        down_shift_total,
    )


def solution(mesh):
    fine = Mesh(mesh.devices.reshape(4, 4, 2, 2, 2), AXES)
    tokens = P(DP, "u", None)
    split_rows = P(AXES, None)
    split_columns = P(None, AXES)
    split_vector = P(AXES)
    return jax.shard_map(
        per_device,
        mesh=fine,
        in_specs=(tokens, tokens, P(DP, "u"), tokens)
        + (split_columns,) * 2
        + (split_rows,) * 7
        + (split_vector, split_rows, split_vector),
        out_specs=(tokens, tokens)
        + (split_columns,) * 2
        + (split_rows,) * 7
        + (split_vector, split_rows, split_vector),
        check_vma=False,
    )
```

```python
import functools

import jax
import jax.numpy as jnp
from jax import lax
from jax.experimental import pallas as pl
from jax.experimental.pallas import tpu as pltpu
from jax.sharding import Mesh, PartitionSpec as P

HEAD = 72
HEADS = 16
BF = jnp.bfloat16
F32 = jnp.float32
AXES = ("z", "x", "v", "c", "u")
DP = ("z", "x", "v", "c")
NAMES = {"z": ("z", "c"), "x": ("x", "c"), "y": ("v", "c", "u")}


WIDE = 640


def dot(left, right):
    return jnp.dot(left, right, preferred_element_type=F32)


def dot_nt(left, right):
    return lax.dot_general(left, right, (((1,), (1,)), ((), ())), preferred_element_type=F32)


def dot_tn(left, right):
    return lax.dot_general(left, right, (((0,), (0,)), ((), ())), preferred_element_type=F32)


def lane_window(head):
    start = head * HEAD
    low = min(start // 128, (HEADS * HEAD) // 128 - 2) * 128
    return slice(low, low + 256), start - low


def head_mask(offset, rows):
    lane = lax.broadcasted_iota(jnp.int32, (rows, 256), 1)
    return (lane >= offset) & (lane < offset + HEAD)


def only(mask, values):
    return jnp.where(mask, values, jnp.zeros_like(values))


def softmax(scores):
    weights = jnp.exp(scores - jnp.max(scores, -1, keepdims=True))
    return weights * (1.0 / jnp.sum(weights, -1, keepdims=True))


def attend_into(total, query_ref, memory_ref, scale):
    tokens, width = query_ref.shape
    total[...] = jnp.zeros_like(total)
    for head in range(HEADS):
        window, offset = lane_window(head)
        beside = slice(window.start + width, window.stop + width)
        mask = head_mask(offset, tokens)
        scores = dot_nt(only(mask, query_ref[:, window]), memory_ref[:, window]) * scale
        mixed = dot(softmax(scores).astype(BF), memory_ref[:, beside])
        total[:, window] += only(mask, mixed)


def attend_back_into(query_total, memory_total, query_ref, memory_ref, upstream_ref, scale):
    tokens, width = query_ref.shape
    query_total[...] = jnp.zeros_like(query_total)
    memory_total[...] = jnp.zeros_like(memory_total)
    for head in range(HEADS):
        window, offset = lane_window(head)
        beside = slice(window.start + width, window.stop + width)
        mask = head_mask(offset, tokens)
        query = only(mask, query_ref[:, window])
        upstream = only(mask, upstream_ref[:, window])
        probs = softmax(dot_nt(query, memory_ref[:, window]) * scale)
        probs_grad = dot_nt(upstream, memory_ref[:, beside])
        memory_total[:, beside] += dot_tn(probs.astype(BF), upstream)
        scores_grad = (
            probs * (probs_grad - jnp.sum(probs * probs_grad, -1, keepdims=True))
        ).astype(BF)
        query_total[:, window] += only(mask, dot(scores_grad, memory_ref[:, window])) * scale
        memory_total[:, window] += dot_tn(scores_grad, query) * scale


def norm_parts(values):
    center = values - jnp.mean(values, -1, keepdims=True)
    inverse = lax.rsqrt(jnp.mean(center * center, -1, keepdims=True) + 1e-05)
    return center * inverse, inverse


def norm_back(values, gain, upstream):
    hat, inverse = norm_parts(values)
    scaled = upstream * gain
    result = inverse * (
        scaled
        - jnp.mean(scaled, -1, keepdims=True)
        - hat * jnp.mean(scaled * hat, -1, keepdims=True)
    )
    return (
        result,
        jnp.sum(upstream * hat, 0, keepdims=True),
        jnp.sum(upstream, 0, keepdims=True),
    )


def fetch(core_ref, when_zero, when_one, target, sem, columns=None):
    def view(ref):
        return ref if columns is None else ref.at[:, columns]

    zero = core_ref[0] == 0

    @pl.when(zero)
    def _():
        pltpu.make_async_copy(view(when_zero), target, sem).start()

    @pl.when(jnp.logical_not(zero))
    def _():
        pltpu.make_async_copy(view(when_one), target, sem).start()

    return pltpu.make_async_copy(view(when_zero), target, sem).wait


def project_kernel(inputs, norms, own, first, mine, theirs, handed, weight, sems):
    tokens = mine.shape[0]
    copy = pltpu.make_async_copy(own.at[:, : weight.shape[1]], weight, sems.at[0])
    copy.start()
    hat, _ = norm_parts(inputs[...].astype(F32))
    first[...] = (hat * norms[0:1] + norms[1:2]).astype(BF)
    copy.wait()
    mine[...] = dot(first[:tokens], weight[...]).astype(BF)
    theirs[...] = dot(first[tokens:], weight[...]).astype(BF)


def attend_kernel(scale, queries, key_values, attended, total):
    attend_into(total, queries, key_values, scale)
    attended[...] = total[...].astype(BF)


def forward_kernel(
    scale, core, attended, inputs, words, norms, mixed_own, mixed_other, own, other,
    second, second_in, cross_queries, cross_out, third, third_in,
    out, cross, ask, total, sems,
):
    width = inputs.shape[1]
    wait_out = fetch(core, mixed_own, mixed_other, out, sems.at[0])
    wait_ask = fetch(core, other, own, ask, sems.at[1], slice(width, 2 * width))
    wait_cross = fetch(core, mixed_other, mixed_own, cross, sems.at[2])
    wait_out()
    value = inputs[...].astype(F32) + dot(attended[...], out[...])
    second[...] = value
    hat, _ = norm_parts(value)
    second_in[...] = (hat * norms[2:3] + norms[3:4]).astype(BF)
    wait_ask()
    cross_queries[...] = dot(second_in[...], ask[...]).astype(BF)
    attend_into(total, cross_queries, words, scale)
    cross_out[...] = total[...].astype(BF)
    wait_cross()
    value = second[...] + dot(cross_out[...], cross[...])
    third[...] = value
    hat, _ = norm_parts(value)
    third_in[...] = (hat * norms[4:5] + norms[5:6]).astype(BF)


def cross_back_kernel(
    scale, core, upstream, third, second, cot, masked, words, cross_queries, norms, mixed_own, mixed_other, own, other,
    cross_branch, cross_query_grad, words_grad, self_branch, second_grad, attended_grad, small,
    out, cross, ask, grad, query_total, words_total, sems,
):
    width = third.shape[1]
    wait_cross = fetch(core, mixed_other, mixed_own, cross, sems.at[2])
    wait_ask = fetch(core, other, own, ask, sems.at[1], slice(width, 2 * width))
    wait_out = fetch(core, mixed_own, mixed_other, out, sems.at[0])
    change, gain, shift = norm_back(third[...], norms[4:5], upstream[...])
    small[...] = jnp.zeros_like(small)
    small[2:3] = gain
    small[5:6] = shift
    value = cot[...].astype(F32) * masked[...] + change
    second_grad[...] = value
    cross_branch[...] = value.astype(BF)
    wait_cross()
    grad[...] = dot_nt(cross_branch[...], cross[...]).astype(BF)
    attend_back_into(query_total, words_total, cross_queries, words, grad, scale)
    cross_query_grad[...] = query_total[...].astype(BF)
    words_grad[...] = words_total[...].astype(BF)
    wait_ask()
    change, gain, shift = norm_back(
        second[...], norms[2:3], dot_nt(cross_query_grad[...], ask[...])
    )
    small[1:2] = gain
    small[4:5] = shift
    value = second_grad[...] + change
    second_grad[...] = value
    self_branch[...] = value.astype(BF)
    wait_out()
    attended_grad[...] = dot_nt(self_branch[...], out[...]).astype(BF)


def attend_back_kernel(
    scale, queries, key_values, attended_grad, query_grad, key_grad, value_grad, key_value_else,
    query_total, key_value_total,
):
    tokens, width = queries.shape
    attend_back_into(query_total, key_value_total, queries, key_values, attended_grad, scale)
    query_grad[...] = query_total[...].astype(BF)
    key_grad[...] = key_value_total[:tokens, :width].astype(BF)
    value_grad[...] = key_value_total[:tokens, width:].astype(BF)
    key_value_else[...] = key_value_total[tokens:].astype(BF)


def late_kernel(core, query_grad, key_grad, value_grad, theirs, cross_query_grad, keys, values, mine, send):
    width = query_grad.shape[1]
    keys[...] = (key_grad[...].astype(F32) + theirs[:, :width].astype(F32)).astype(BF)
    values[...] = (value_grad[...].astype(F32) + theirs[:, width:].astype(F32)).astype(BF)

    def store(zero_ref, one_ref):
        zero_ref[:, :width] = query_grad[...]
        zero_ref[:, width:] = keys[...]
        one_ref[:, :width] = values[...]
        one_ref[:, width:] = cross_query_grad[...]

    zero = core[0] == 0

    @pl.when(zero)
    def _():
        store(mine, send)

    @pl.when(jnp.logical_not(zero))
    def _():
        store(send, mine)


def input_kernel(
    core, query_grad, key_grad, value_grad, inputs, second_grad, norms, own, other, input_grad, small, both, side, sems
):
    width = inputs.shape[1]
    wait_both = fetch(core, own, other, both, sems.at[0], slice(0, 2 * width))
    wait_side = fetch(core, other, own, side, sems.at[1], slice(0, width))
    wait_both()
    upstream = dot_nt(query_grad[...], both[:, :width]) + dot_nt(key_grad[...], both[:, width:])
    wait_side()
    upstream = upstream + dot_nt(value_grad[...], side[...])
    change, gain, shift = norm_back(inputs[...].astype(F32), norms[0:1], upstream)
    input_grad[...] = second_grad[...] + change
    small[...] = jnp.zeros_like(small)
    small[0:1] = gain
    small[1:2] = shift


def finish_kernel(parts, joined, query, out, cross):
    rows, width = out.shape
    halves = []
    for half in range(2):
        value = 0.0
        for v in range(2):
            for u in range(2):
                value = value + parts[4 * v + 2 * half + u][:rows, : 3 * width].astype(F32)
        halves.append(value)
    zero, one = halves
    joined[:, : 2 * width] = zero[:, : 2 * width]
    joined[:, 2 * width :] = one[:, :width]
    query[...] = one[:, width : 2 * width]
    out[...] = zero[:, 2 * width :]
    cross[...] = one[:, 2 * width :]


def unpack_kernel(packed, up, down):
    part, width = down.shape
    up[...] = packed[:, width : width + part]
    values = packed[:, width + WIDE :].astype(F32)
    block, down_block = width // 16, part // 16
    for index in range(16):
        rows = slice(index * down_block, (index + 1) * down_block)
        start = index * block
        down[rows, :WIDE] = values[start : start + down_block].astype(BF)
        down[rows, width - WIDE :] = values[start + down_block : start + block].astype(BF)


def feed_forward_kernel(third, upward_grad, hidden, branch, out):
    part = hidden.shape[1]
    block, down_block = third.shape[1] // 16, part // 16
    up = dot_tn(third[...], upward_grad[...])
    out[:, :, part : WIDE] = jnp.zeros((16, block, WIDE - part), BF)
    out[:, :, WIDE + part :] = jnp.zeros((16, block, WIDE - part), BF)
    for index in range(16):
        out[index, :, :part] = up[index * block : (index + 1) * block].astype(BF)
    for half in range(2):
        down = dot_tn(hidden[...], branch[:, half * part : (half + 1) * part])
        for index in range(16):
            out[index, half * down_block : (half + 1) * down_block, WIDE : WIDE + part] = down[
                index * down_block : (index + 1) * down_block
            ].astype(BF)


def call(kernel, ins, outs, scratch, earlier=(), moved=1, handed=None):
    spaces = {"v": pltpu.VMEM, "s": pltpu.SMEM, "a": pl.ANY}
    held = jax.tree.leaves(earlier)
    count = len(ins)
    last = [] if handed is None else [handed]
    outs = outs + [(ins[index][0].shape, ins[index][0].dtype) for index in last]

    def body(*refs):
        kernel(*refs[:count], *refs[count + len(held) :])

    return pl.pallas_call(
        body,
        in_specs=[pl.BlockSpec(memory_space=spaces[space]) for _, space in ins]
        + [pl.BlockSpec(memory_space=pl.ANY)] * len(held),
        out_specs=[pl.BlockSpec(memory_space=pltpu.VMEM) for _ in outs[: len(outs) - len(last)]]
        + [pl.BlockSpec(memory_space=pl.ANY)] * len(last),
        out_shape=[jax.ShapeDtypeStruct(shape, dtype) for shape, dtype in outs],
        input_output_aliases={index: len(outs) - 1 for index in last},
        scratch_shapes=scratch,
        cost_estimate=pl.CostEstimate(flops=1, bytes_accessed=moved, transcendentals=0),
        compiler_params=pltpu.CompilerParams(vmem_limit_bytes=56 * 2**20),
    )(*[array for array, _ in ins], *held)


def weight_gradient(lefts, mine, theirs, start, total, base=None, earlier=()):
    parts, tokens, rows = lefts.shape
    columns = mine.shape[1]
    tile = 384
    steps = columns // parts // tile
    held = ([] if base is None else [base]) + jax.tree.leaves(earlier)

    def body(lefts_ref, mine_ref, theirs_ref, *refs):
        half = tokens // 2
        value = dot_tn(lefts_ref[0, :half], mine_ref[...])
        refs[-1][...] = (value + dot_tn(lefts_ref[0, half:], theirs_ref[...])).astype(BF)

    return pl.pallas_call(
        body,
        grid=(parts * steps,),
        in_specs=[
            pl.BlockSpec((1, tokens, rows), lambda step: (step // steps, 0, 0)),
            pl.BlockSpec((tokens // 2, tile), lambda step: (0, step)),
            pl.BlockSpec((tokens // 2, tile), lambda step: (0, step)),
        ]
        + [pl.BlockSpec(memory_space=pl.ANY)] * len(held),
        out_specs=pl.BlockSpec((rows, tile), lambda step: (0, step + start // tile)),
        out_shape=jax.ShapeDtypeStruct((rows, total), BF),
        input_output_aliases={} if base is None else {3: 0},
        cost_estimate=pl.CostEstimate(flops=1, bytes_accessed=1, transcendentals=0),
        compiler_params=pltpu.CompilerParams(vmem_limit_bytes=56 * 2**20),
    )(lefts, mine, theirs, *held)


def after(values, *earlier):
    flat, tree = jax.tree.flatten(values)
    held = jax.tree.leaves(earlier)
    outs = pl.pallas_call(
        lambda *refs: None,
        in_specs=[pl.BlockSpec(memory_space=pl.ANY)] * (len(flat) + len(held)),
        out_specs=[pl.BlockSpec(memory_space=pl.ANY)] * len(flat),
        out_shape=[jax.ShapeDtypeStruct(value.shape, value.dtype) for value in flat],
        input_output_aliases={index: index for index in range(len(flat))},
        cost_estimate=pl.CostEstimate(flops=1, bytes_accessed=1, transcendentals=0),
    )(*flat, *held)
    return jax.tree.unflatten(tree, outs)


def swap(value):
    return lax.ppermute(value, "c", [(0, 1), (1, 0)])


def position_index(axis, place, core):
    if axis == "y":
        return ((place % 2) * 2 + core) * 2 + place // 2
    return place * 2 + core


def receive(value, axis, step, mirrored=True):
    pairs = []
    for core in range(2):
        own = -step if mirrored and core == 1 else step
        for place in range(4):
            pairs.append(
                (position_index(axis, (place + own) % 4, core), position_index(axis, place, core))
            )
    return lax.ppermute(value, NAMES[axis], pairs)


def place_of(axis):
    if axis == "y":
        return 2 * lax.axis_index("u") + lax.axis_index("v")
    return lax.axis_index(axis)


def sign_of():
    return 1 - 2 * lax.axis_index("c")


def places(axis):
    here, sign = place_of(axis), sign_of()
    mine = [here, (here + sign) % 4, (here - sign) % 4, (here + 2) % 4]
    return mine, [mine[0], mine[2], mine[1], mine[3]]


def by_place(pieces, spots):
    slots = jnp.arange(4).reshape((4,) + (1,) * pieces[0].ndim)
    out = pieces[3][None]
    for piece, spot in zip(pieces[:3], spots[:3]):
        out = jnp.where(slots == spot, piece[None], out)
    return out


def gather_direct(value, axis):
    return [
        value,
        receive(value, axis, 1),
        receive(value, axis, -1),
        receive(value, axis, 2, False),
    ]


def scatter(pieces, axis, earlier=()):
    own, first, second, far = pieces
    came = [
        receive(first.astype(BF), axis, -1),
        receive(second.astype(BF), axis, 1),
        receive(far.astype(BF), axis, 2, False),
    ]
    if earlier:
        came = after(came, *earlier)
    return own.astype(F32) + sum(piece.astype(F32) for piece in came)


def exchange(blocks, axes):
    return lax.all_to_all(blocks, axes, 0, 0, tiled=True)


def spread(value, axes, count):
    return exchange(jnp.broadcast_to(value[None], (count,) + value.shape), axes)


def exchange_sum(blocks, axes):
    return jnp.sum(exchange(blocks.astype(BF), axes).astype(F32), 0)


def gather_plane(value):
    return lax.all_gather(value, ("z", "x"), axis=0, tiled=True)


def scatter_plane(value, axes=("z", "x")):
    blocks = value.reshape(16, value.shape[0] // 16, value.shape[1])
    return lax.psum_scatter(blocks, axes, scatter_dimension=0, tiled=True)[0]


def pair_one(when_zero, when_one):
    zero = lax.axis_index("c") == 0
    return jnp.concatenate(
        [jnp.where(zero, when_zero, when_one), swap(jnp.where(zero, when_one, when_zero))], -2
    )


def per_device(
    inputs,
    text,
    masked,
    cot,
    norm_gains,
    norm_biases,
    w_qkv,
    w_out,
    w_text,
    w_query,
    w_memory,
    w_cross_out,
    w_up,
    up_bias,
    w_down,
    down_bias,
):
    inputs, text, masked, cot = inputs[0], text[0], masked[0], cot[0]
    tokens, width = inputs.shape
    half_words = text.shape[0]
    wide = w_up.shape[1]
    part = wide // 8
    rows = w_qkv.shape[0]
    text_rows, down_rows = w_text.shape[0], w_down.shape[0]
    scale = HEAD ** (-0.5)
    core = lax.axis_index("c")
    zero = core == 0
    core_word = core.astype(jnp.int32).reshape(1)
    group = ("v", "c", "u")
    inputs_both = jnp.concatenate([inputs, swap(inputs)], 0)

    extra = jnp.concatenate(
        [
            jnp.stack([norm_gains, norm_biases], 1).reshape(6, rows).T,
            up_bias.reshape(rows, -1),
            down_bias[:, None],
        ],
        1,
    )
    extra = jnp.pad(extra, ((0, 0), (0, 128 - extra.shape[1])))
    halves = jnp.stack(
        [
            jnp.concatenate([w_qkv[:, : 2 * width], extra, w_out], 1),
            jnp.concatenate([w_qkv[:, 2 * width :], w_query, extra, w_cross_out], 1),
        ]
    )
    half_columns = halves.shape[-1]
    halves = jnp.broadcast_to(halves[None, :, None], (2, 2, 2) + halves.shape[1:])
    eighths = w_up.reshape(rows, 16, 8, down_rows).transpose(2, 0, 1, 3).reshape(8, rows, part)
    columns = half_columns + WIDE
    words = text.reshape(half_words, 16, 8, text_rows).transpose(2, 0, 1, 3).reshape(8, 2, -1)
    parts = jnp.concatenate(
        [
            jnp.concatenate(
                [
                    halves.reshape(8, rows, half_columns),
                    jnp.pad(eighths, ((0, 0), (0, 0), (0, WIDE - part))),
                ],
                2,
            ),
            jnp.pad(words, ((0, 0), (0, 0), (0, columns - words.shape[2]))),
        ],
        1,
    )
    parts = exchange(parts, group)
    joined_columns = 2 * width + 128
    own = gather_plane(parts[:, :rows, :joined_columns].reshape(8 * rows, joined_columns))
    text_all = parts[:, rows:, : words.shape[2]].reshape(8 * half_words, 16 * text_rows)

    sorted_text = w_text.reshape(text_rows, 16, 8, rows).transpose(0, 2, 1, 3).reshape(text_rows, width)
    slab = jnp.concatenate([sorted_text, w_memory.reshape(2 * rows, width)], 0)
    slab = by_place(gather_direct(slab, "x"), places("x")[0])
    slab = by_place(gather_direct(slab, "z"), places("z")[0]).reshape(16, -1, width)
    text_weight = slab[:, :text_rows].reshape(-1, width)
    memory_weight = slab[:, text_rows:].reshape(16 * rows, 2 * width)

    packed = jnp.concatenate(
        [
            parts[:, :rows, joined_columns:].reshape(8 * rows, width + WIDE),
            jnp.concatenate([w_down[:, :WIDE], w_down[:, width - WIDE :]], 0),
        ],
        1,
    )
    packed = gather_plane(packed)

    def other_half(values):
        return lax.ppermute(values, "u", [(0, 1), (1, 0)])

    def both_cores(ring):
        ring = jnp.concatenate(ring, 0)
        return jnp.concatenate([ring, swap(ring)], 0)

    def fold_tokens(values):
        ring = values[: 4 * tokens] + swap(values[4 * tokens :].astype(BF)).astype(F32)
        return [ring[index * tokens : (index + 1) * tokens] for index in range(4)]

    projected = dot(text_all, text_weight).reshape(8 * half_words, 8, 16 * rows).transpose(1, 0, 2)
    projected = exchange_sum(projected, group).astype(BF)
    loss_tokens = masked.astype(F32)[:, None]
    branch = (cot.astype(F32) * loss_tokens).astype(BF)
    branch_all = both_cores(gather_direct(after(branch, text_all), "y"))
    down_shift_grad = jnp.sum(branch.astype(F32), 0)
    own = after(own, branch_all, projected)
    shifts = own[:, 2 * width : 2 * width + 128].astype(F32)
    norms = shifts[:, :6].T

    first, mine, theirs, own = call(
        project_kernel,
        [(inputs_both, "v"), (norms, "v"), (own, "a")],
        [((2 * tokens, width), BF), ((tokens, 2 * width), BF), ((tokens, 2 * width), BF)],
        [pltpu.VMEM((width, 2 * width), BF), pltpu.SemaphoreType.DMA((1,))],
        handed=2,
    )
    theirs = swap(theirs)
    queries = jnp.where(zero, mine[:, :width], theirs[:, :width])
    key_value = jnp.concatenate(
        [
            jnp.where(zero, mine[:, width:], theirs[:, width:]),
            jnp.where(zero, theirs[:, :width], mine[:, :width]),
        ],
        1,
    )
    own = after(own, key_value)
    other = swap(own)
    key_value = jnp.concatenate([key_value, other_half(key_value)], 0)
    projected = after(projected, key_value)
    words = dot(projected, memory_weight).reshape(4, 1, 2 * half_words, 2 * width)
    words = jnp.broadcast_to(words, (4, 2) + words.shape[2:]).reshape(8, 2 * half_words, 2 * width)
    words = exchange(words.astype(BF), group)
    attended = call(
        functools.partial(attend_kernel, scale),
        [(queries, "v"), (key_value, "v")],
        [((tokens, width), BF)],
        [pltpu.VMEM((tokens, width), F32)],
    )[0]
    packed, words = after((packed, words), attended)
    mixed_own = packed[:, :width]
    words = jnp.sum(words.astype(F32), 0).astype(BF)
    mixed_other = swap(mixed_own)
    weights = [(value, "a") for value in (mixed_own, mixed_other, own, other)]
    second, second_in, cross_queries, cross_out, third, third_in = call(
        functools.partial(forward_kernel, scale),
        [(core_word, "s"), (attended, "v"), (inputs, "v"), (words, "v"), (norms, "v")]
        + weights,
        [
            ((tokens, width), F32),
            ((tokens, width), BF),
            ((tokens, width), BF),
            ((tokens, width), BF),
            ((tokens, width), F32),
            ((tokens, width), BF),
        ],
        [
            pltpu.VMEM((width, width), BF),
            pltpu.VMEM((width, width), BF),
            pltpu.VMEM((width, width), BF),
            pltpu.VMEM((tokens, width), F32),
            pltpu.SemaphoreType.DMA((3,)),
        ],
    )
    shifts = after(shifts, third_in)
    place = (lax.axis_index("v") * 2 + core) * 2 + lax.axis_index("u")
    up_shift = lax.dynamic_index_in_dim(
        shifts[:, 6:10].reshape(16, 8, down_rows), place, 1, False
    ).reshape(part)
    down_shift = shifts[:, 10]
    up_weight, down_weight = call(
        unpack_kernel,
        [(packed, "v")],
        [((width, part), BF), ((part, width), BF)],
        [],
        [third_in],
    )

    third_all = both_cores(gather_direct(third_in, "y"))
    hidden_grad = dot_nt(branch_all, down_weight)
    upward = dot(third_all, up_weight) + up_shift
    upward_grad = jax.vjp(jax.nn.gelu, upward)[1](hidden_grad)[0].astype(BF)
    hidden = jax.nn.gelu(upward).astype(BF)
    third_in_grad = fold_tokens(dot_nt(upward_grad, up_weight))
    up_down_grad = call(
        feed_forward_kernel,
        [(third_all, "v"), (upward_grad, "v"), (hidden, "v"), (branch_all, "v")],
        [((16, 8 * rows, 2 * WIDE), BF)],
        [],
        third_in_grad,
        1,
    )[0]
    third_in_grad = scatter(third_in_grad, "y", [up_down_grad])
    up_down_total = lax.psum_scatter(
        up_down_grad, ("z", "x"), scatter_dimension=0, tiled=True
    )[0].astype(F32)
    up_shift_grad = jnp.sum(upward_grad.astype(F32), 0)

    (
        cross_branch,
        cross_query_grad,
        words_grad,
        self_branch,
        second_grad,
        attended_grad,
        norm_grads,
    ) = call(
        functools.partial(cross_back_kernel, scale),
        [
            (core_word, "s"),
            (third_in_grad, "v"),
            (third, "v"),
            (second, "v"),
            (cot, "v"),
            (loss_tokens, "v"),
            (words, "v"),
            (cross_queries, "v"),
            (norms, "v"),
        ]
        + weights,
        [
            ((tokens, width), BF),
            ((tokens, width), BF),
            ((2 * half_words, 2 * width), BF),
            ((tokens, width), BF),
            ((tokens, width), F32),
            ((tokens, width), BF),
            ((8, width), F32),
        ],
        [
            pltpu.VMEM((width, width), BF),
            pltpu.VMEM((width, width), BF),
            pltpu.VMEM((width, width), BF),
            pltpu.VMEM((tokens, width), BF),
            pltpu.VMEM((tokens, width), F32),
            pltpu.VMEM((2 * half_words, 2 * width), F32),
            pltpu.SemaphoreType.DMA((3,)),
        ],
        [up_down_grad],
    )
    query_grad, key_grad, value_grad, key_value_else = call(
        functools.partial(attend_back_kernel, scale),
        [(queries, "v"), (key_value, "v"), (attended_grad, "v")],
        [
            ((tokens, width), BF),
            ((tokens, width), BF),
            ((tokens, width), BF),
            ((tokens, 2 * width), BF),
        ],
        [pltpu.VMEM((tokens, width), F32), pltpu.VMEM((2 * tokens, 2 * width), F32)],
    )
    words_grad = spread(words_grad, group, 8).reshape(4, 2, 2 * half_words, 2 * width)
    words_grad = jnp.sum(words_grad.astype(F32), 1).reshape(8 * half_words, 2 * width).astype(BF)
    projected_grad = spread(
        dot_nt(after(words_grad, key_value_else), memory_weight).astype(BF), group, 8
    )
    projected_grad = projected_grad.transpose(1, 0, 2).reshape(8 * half_words, width)

    attention_columns = 3 * width
    branch_mine = jnp.where(zero, self_branch, cross_branch)
    branch_theirs = swap(jnp.where(zero, cross_branch, self_branch))
    first_right = jnp.where(zero, first, pair_one(second_in, second_in))
    attention_grad = weight_gradient(
        pair_one(attended, cross_out)[None],
        branch_mine,
        branch_theirs,
        2 * width,
        attention_columns,
        earlier=[key_value_else, first_right],
    )
    key_grad, value_grad, mine, send = call(
        late_kernel,
        [
            (core_word, "s"),
            (query_grad, "v"),
            (key_grad, "v"),
            (value_grad, "v"),
            (other_half(key_value_else), "v"),
            (cross_query_grad, "v"),
        ],
        [((tokens, width), BF)] * 2 + [((tokens, 2 * width), BF)] * 2,
        [],
        [attention_grad],
    )
    attention_grad = weight_gradient(
        jnp.stack([first, first_right]),
        mine,
        swap(send),
        0,
        attention_columns,
        attention_grad,
    )

    input_grads, last_grads = call(
        input_kernel,
        [
            (core_word, "s"),
            (query_grad, "v"),
            (key_grad, "v"),
            (value_grad, "v"),
            (inputs, "v"),
            (second_grad, "v"),
            (norms, "v"),
        ]
        + weights[2:],
        [((tokens, width), F32), ((8, width), F32)],
        [
            pltpu.VMEM((width, 2 * width), BF),
            pltpu.VMEM((width, width), BF),
            pltpu.SemaphoreType.DMA((2,)),
        ],
        [attention_grad],
    )
    projected_grad = after(projected_grad, attention_grad)
    slab_grad = jnp.concatenate(
        [
            dot_tn(text_all, projected_grad).reshape(16, text_rows, width),
            dot_tn(projected, words_grad).reshape(16, 2 * rows, width),
        ],
        1,
    )

    final = third + scatter(
        fold_tokens(dot(after(hidden, attention_grad), down_weight)), "y"
    ) + down_shift
    block_output = final.astype(BF)

    down_total = jnp.concatenate(
        [
            up_down_total[:down_rows, WIDE : WIDE + part],
            up_down_total[down_rows:, WIDE : WIDE + part],
        ],
        1,
    )
    by_place_part = jnp.where(
        jnp.arange(8)[None, :, None] == place, up_shift_grad.reshape(16, 1, down_rows), 0.0
    ).reshape(128, down_rows)
    gain_terms = jnp.concatenate([last_grads[:1], norm_grads[1:3]], 0)
    shift_terms = jnp.concatenate([last_grads[1:2], norm_grads[4:6]], 0)
    small_grads = jnp.concatenate(
        [
            gain_terms.reshape(3, 128, rows).transpose(1, 0, 2).reshape(128, 3 * rows),
            shift_terms.reshape(3, 128, rows).transpose(1, 0, 2).reshape(128, 3 * rows),
            by_place_part,
            down_shift_grad.reshape(128, rows),
        ],
        1,
    )

    def split(values):
        high = values.astype(BF)
        return high, (values - high.astype(F32)).astype(BF)

    count = small_grads.shape[1]
    small_grads = jnp.pad(
        small_grads.reshape(16, 8, count), ((0, 0), (0, 0), (0, 8 * rows * 2 - count))
    ).reshape(16, width)
    slab_grad = jnp.concatenate([slab_grad.astype(BF), jnp.stack(split(small_grads), 1)], 1)
    slab_total = exchange_sum(slab_grad, ("z", "x"))
    text_total = (
        slab_total[:text_rows]
        .reshape(text_rows, 8, 16, rows)
        .transpose(0, 2, 1, 3)
        .reshape(text_rows, width)
    )
    memory_total = slab_total[text_rows:-2].reshape(rows, 2 * width)
    small_total = split(jnp.sum(slab_total[-2:], 0).reshape(8, 1, -1))

    total = scatter_plane(attention_grad).reshape(8, rows, -1)
    total = jnp.concatenate(
        [
            jnp.concatenate([total, up_down_total[:, :WIDE].astype(BF).reshape(8, rows, WIDE)], 2),
            jnp.pad(
                jnp.concatenate(small_total, 2),
                ((0, 0), (0, 0), (0, attention_columns + WIDE - 2 * small_total[0].shape[2])),
            ),
        ],
        1,
    )
    total = exchange(total, group)
    joined_total, query_total, out_total, cross_total_grad = call(
        finish_kernel,
        [(total, "v")],
        [((rows, 3 * width), F32)] + [((rows, width), F32)] * 3,
        [],
    )
    up_total = (
        total[:, :rows, attention_columns : attention_columns + part]
        .reshape(8, rows, 16, down_rows)
        .transpose(1, 2, 0, 3)
        .reshape(rows, wide)
        .astype(F32)
    )
    small_total = jnp.sum(total[:, rows].astype(F32), 0)
    small_total = small_total[:count] + small_total[16 * rows : 16 * rows + count]
    gain_total = small_total[: 3 * rows].reshape(3, rows)
    shift_total = small_total[3 * rows : 6 * rows].reshape(3, rows)
    up_shift_total = small_total[6 * rows : 6 * rows + down_rows]
    down_shift_total = small_total[6 * rows + down_rows :]
    return (
        block_output[None],
        input_grads[None],
        gain_total,
        shift_total,
        joined_total,
        out_total,
        text_total,
        query_total,
        memory_total,
        cross_total_grad,
        up_total,
        up_shift_total,
        down_total,
        down_shift_total,
    )


def solution(mesh):
    fine = Mesh(mesh.devices.reshape(4, 4, 2, 2, 2), AXES)
    tokens = P(DP, "u", None)
    split_rows = P(AXES, None)
    split_columns = P(None, AXES)
    split_vector = P(AXES)
    return jax.shard_map(
        per_device,
        mesh=fine,
        in_specs=(tokens, tokens, P(DP, "u"), tokens)
        + (split_columns,) * 2
        + (split_rows,) * 7
        + (split_vector, split_rows, split_vector),
        out_specs=(tokens, tokens)
        + (split_columns,) * 2
        + (split_rows,) * 7
        + (split_vector, split_rows, split_vector),
        check_vma=False,
    )
```

```python
import functools

import jax
import jax.numpy as jnp
from jax import lax
from jax.experimental import pallas as pl
from jax.experimental.pallas import tpu as pltpu
from jax.sharding import Mesh, PartitionSpec as P

HEAD = 72
HEADS = 16
BF = jnp.bfloat16
F32 = jnp.float32
AXES = ("z", "x", "v", "c", "u")
DP = ("z", "x", "v", "c")
NAMES = {"z": ("z", "c"), "x": ("x", "c"), "y": ("v", "c", "u")}


WIDE = 640


def dot(left, right):
    return jnp.dot(left, right, preferred_element_type=F32)


def dot_nt(left, right):
    return lax.dot_general(left, right, (((1,), (1,)), ((), ())), preferred_element_type=F32)


def dot_tn(left, right):
    return lax.dot_general(left, right, (((0,), (0,)), ((), ())), preferred_element_type=F32)


def lane_window(head):
    start = head * HEAD
    low = min(start // 128, (HEADS * HEAD) // 128 - 2) * 128
    return slice(low, low + 256), start - low


def head_mask(offset, rows):
    lane = lax.broadcasted_iota(jnp.int32, (rows, 256), 1)
    return (lane >= offset) & (lane < offset + HEAD)


def only(mask, values):
    return jnp.where(mask, values, jnp.zeros_like(values))


def softmax(scores):
    weights = jnp.exp(scores - jnp.max(scores, -1, keepdims=True))
    return weights * (1.0 / jnp.sum(weights, -1, keepdims=True))


def attend_into(total, query_ref, memory_ref, scale):
    tokens, width = query_ref.shape
    total[...] = jnp.zeros_like(total)
    for head in range(HEADS):
        window, offset = lane_window(head)
        beside = slice(window.start + width, window.stop + width)
        mask = head_mask(offset, tokens)
        scores = dot_nt(only(mask, query_ref[:, window]), memory_ref[:, window]) * scale
        mixed = dot(softmax(scores).astype(BF), memory_ref[:, beside])
        total[:, window] += only(mask, mixed)


def attend_back_into(query_total, memory_total, query_ref, memory_ref, upstream_ref, scale):
    tokens, width = query_ref.shape
    query_total[...] = jnp.zeros_like(query_total)
    memory_total[...] = jnp.zeros_like(memory_total)
    for head in range(HEADS):
        window, offset = lane_window(head)
        beside = slice(window.start + width, window.stop + width)
        mask = head_mask(offset, tokens)
        query = only(mask, query_ref[:, window])
        upstream = only(mask, upstream_ref[:, window])
        probs = softmax(dot_nt(query, memory_ref[:, window]) * scale)
        probs_grad = dot_nt(upstream, memory_ref[:, beside])
        memory_total[:, beside] += dot_tn(probs.astype(BF), upstream)
        scores_grad = (
            probs * (probs_grad - jnp.sum(probs * probs_grad, -1, keepdims=True))
        ).astype(BF)
        query_total[:, window] += only(mask, dot(scores_grad, memory_ref[:, window])) * scale
        memory_total[:, window] += dot_tn(scores_grad, query) * scale


def norm_parts(values):
    center = values - jnp.mean(values, -1, keepdims=True)
    inverse = lax.rsqrt(jnp.mean(center * center, -1, keepdims=True) + 1e-05)
    return center * inverse, inverse


def norm_back(values, gain, upstream):
    hat, inverse = norm_parts(values)
    scaled = upstream * gain
    result = inverse * (
        scaled
        - jnp.mean(scaled, -1, keepdims=True)
        - hat * jnp.mean(scaled * hat, -1, keepdims=True)
    )
    return (
        result,
        jnp.sum(upstream * hat, 0, keepdims=True),
        jnp.sum(upstream, 0, keepdims=True),
    )


def fetch(core_ref, when_zero, when_one, target, sem, columns=None):
    def view(ref):
        return ref if columns is None else ref.at[:, columns]

    zero = core_ref[0] == 0

    @pl.when(zero)
    def _():
        pltpu.make_async_copy(view(when_zero), target, sem).start()

    @pl.when(jnp.logical_not(zero))
    def _():
        pltpu.make_async_copy(view(when_one), target, sem).start()

    return pltpu.make_async_copy(view(when_zero), target, sem).wait


def project_kernel(inputs, norms, own, first, mine, theirs, handed, weight, sems):
    tokens = mine.shape[0]
    copy = pltpu.make_async_copy(own.at[:, : weight.shape[1]], weight, sems.at[0])
    copy.start()
    hat, _ = norm_parts(inputs[...].astype(F32))
    first[...] = (hat * norms[0:1] + norms[1:2]).astype(BF)
    copy.wait()
    mine[...] = dot(first[:tokens], weight[...]).astype(BF)
    theirs[...] = dot(first[tokens:], weight[...]).astype(BF)


def attend_kernel(scale, queries, key_values, attended, total):
    attend_into(total, queries, key_values, scale)
    attended[...] = total[...].astype(BF)


def forward_kernel(
    scale, core, attended, inputs, words, norms, mixed_own, mixed_other, own, other,
    second, second_in, cross_queries, cross_out, third, third_in,
    out, cross, ask, total, sems,
):
    width = inputs.shape[1]
    wait_out = fetch(core, mixed_own, mixed_other, out, sems.at[0])
    wait_ask = fetch(core, other, own, ask, sems.at[1], slice(width, 2 * width))
    wait_cross = fetch(core, mixed_other, mixed_own, cross, sems.at[2])
    wait_out()
    value = inputs[...].astype(F32) + dot(attended[...], out[...])
    second[...] = value
    hat, _ = norm_parts(value)
    second_in[...] = (hat * norms[2:3] + norms[3:4]).astype(BF)
    wait_ask()
    cross_queries[...] = dot(second_in[...], ask[...]).astype(BF)
    attend_into(total, cross_queries, words, scale)
    cross_out[...] = total[...].astype(BF)
    wait_cross()
    value = second[...] + dot(cross_out[...], cross[...])
    third[...] = value
    hat, _ = norm_parts(value)
    third_in[...] = (hat * norms[4:5] + norms[5:6]).astype(BF)


def cross_back_kernel(
    scale, core, upstream, third, second, cot, masked, words, cross_queries, norms, mixed_own, mixed_other, own, other,
    cross_branch, cross_query_grad, words_grad, self_branch, second_grad, attended_grad, small,
    out, cross, ask, grad, query_total, words_total, sems,
):
    width = third.shape[1]
    wait_cross = fetch(core, mixed_other, mixed_own, cross, sems.at[2])
    wait_ask = fetch(core, other, own, ask, sems.at[1], slice(width, 2 * width))
    wait_out = fetch(core, mixed_own, mixed_other, out, sems.at[0])
    change, gain, shift = norm_back(third[...], norms[4:5], upstream[...])
    small[...] = jnp.zeros_like(small)
    small[2:3] = gain
    small[5:6] = shift
    value = cot[...].astype(F32) * masked[...] + change
    second_grad[...] = value
    cross_branch[...] = value.astype(BF)
    wait_cross()
    grad[...] = dot_nt(cross_branch[...], cross[...]).astype(BF)
    attend_back_into(query_total, words_total, cross_queries, words, grad, scale)
    cross_query_grad[...] = query_total[...].astype(BF)
    words_grad[...] = words_total[...].astype(BF)
    wait_ask()
    change, gain, shift = norm_back(
        second[...], norms[2:3], dot_nt(cross_query_grad[...], ask[...])
    )
    small[1:2] = gain
    small[4:5] = shift
    value = second_grad[...] + change
    second_grad[...] = value
    self_branch[...] = value.astype(BF)
    wait_out()
    attended_grad[...] = dot_nt(self_branch[...], out[...]).astype(BF)


def attend_back_kernel(
    scale, queries, key_values, attended_grad, query_grad, key_grad, value_grad, key_value_else,
    query_total, key_value_total,
):
    tokens, width = queries.shape
    attend_back_into(query_total, key_value_total, queries, key_values, attended_grad, scale)
    query_grad[...] = query_total[...].astype(BF)
    key_grad[...] = key_value_total[:tokens, :width].astype(BF)
    value_grad[...] = key_value_total[:tokens, width:].astype(BF)
    key_value_else[...] = key_value_total[tokens:].astype(BF)


def late_kernel(core, query_grad, key_grad, value_grad, theirs, cross_query_grad, keys, values, mine, send):
    width = query_grad.shape[1]
    keys[...] = (key_grad[...].astype(F32) + theirs[:, :width].astype(F32)).astype(BF)
    values[...] = (value_grad[...].astype(F32) + theirs[:, width:].astype(F32)).astype(BF)

    def store(zero_ref, one_ref):
        zero_ref[:, :width] = query_grad[...]
        zero_ref[:, width:] = keys[...]
        one_ref[:, :width] = values[...]
        one_ref[:, width:] = cross_query_grad[...]

    zero = core[0] == 0

    @pl.when(zero)
    def _():
        store(mine, send)

    @pl.when(jnp.logical_not(zero))
    def _():
        store(send, mine)


def input_kernel(
    core, query_grad, key_grad, value_grad, inputs, second_grad, norms, own, other, input_grad, small, both, side, sems
):
    width = inputs.shape[1]
    wait_both = fetch(core, own, other, both, sems.at[0], slice(0, 2 * width))
    wait_side = fetch(core, other, own, side, sems.at[1], slice(0, width))
    wait_both()
    upstream = dot_nt(query_grad[...], both[:, :width]) + dot_nt(key_grad[...], both[:, width:])
    wait_side()
    upstream = upstream + dot_nt(value_grad[...], side[...])
    change, gain, shift = norm_back(inputs[...].astype(F32), norms[0:1], upstream)
    input_grad[...] = second_grad[...] + change
    small[...] = jnp.zeros_like(small)
    small[0:1] = gain
    small[1:2] = shift


def finish_kernel(parts, joined, query, out, cross):
    rows, width = out.shape
    halves = []
    for half in range(2):
        value = 0.0
        for v in range(2):
            for u in range(2):
                value = value + parts[4 * v + 2 * half + u][:rows, : 3 * width].astype(F32)
        halves.append(value)
    zero, one = halves
    joined[:, : 2 * width] = zero[:, : 2 * width]
    joined[:, 2 * width :] = one[:, :width]
    query[...] = one[:, width : 2 * width]
    out[...] = zero[:, 2 * width :]
    cross[...] = one[:, 2 * width :]


def unpack_kernel(packed, up, down):
    part, width = down.shape
    up[...] = packed[:, width : width + part]
    values = packed[:, width + WIDE :].astype(F32)
    block, down_block = width // 16, part // 16
    for index in range(16):
        rows = slice(index * down_block, (index + 1) * down_block)
        start = index * block
        down[rows, :WIDE] = values[start : start + down_block].astype(BF)
        down[rows, width - WIDE :] = values[start + down_block : start + block].astype(BF)


def feed_forward_kernel(third, upward_grad, hidden, branch, out):
    part = hidden.shape[1]
    block, down_block = third.shape[1] // 16, part // 16
    up = dot_tn(third[...], upward_grad[...])
    out[:, :, part : WIDE] = jnp.zeros((16, block, WIDE - part), BF)
    out[:, :, WIDE + part :] = jnp.zeros((16, block, WIDE - part), BF)
    for index in range(16):
        out[index, :, :part] = up[index * block : (index + 1) * block].astype(BF)
    down = dot_tn(hidden[...], branch[...])
    for index in range(16):
        rows = slice(index * down_block, (index + 1) * down_block)
        for half in range(2):
            out[index, half * down_block : (half + 1) * down_block, WIDE : WIDE + part] = down[
                rows, half * part : (half + 1) * part
            ].astype(BF)


def call(kernel, ins, outs, scratch, earlier=(), moved=1, handed=None):
    spaces = {"v": pltpu.VMEM, "s": pltpu.SMEM, "a": pl.ANY}
    held = jax.tree.leaves(earlier)
    count = len(ins)
    last = [] if handed is None else [handed]
    outs = outs + [(ins[index][0].shape, ins[index][0].dtype) for index in last]

    def body(*refs):
        kernel(*refs[:count], *refs[count + len(held) :])

    return pl.pallas_call(
        body,
        in_specs=[pl.BlockSpec(memory_space=spaces[space]) for _, space in ins]
        + [pl.BlockSpec(memory_space=pl.ANY)] * len(held),
        out_specs=[pl.BlockSpec(memory_space=pltpu.VMEM) for _ in outs[: len(outs) - len(last)]]
        + [pl.BlockSpec(memory_space=pl.ANY)] * len(last),
        out_shape=[jax.ShapeDtypeStruct(shape, dtype) for shape, dtype in outs],
        input_output_aliases={index: len(outs) - 1 for index in last},
        scratch_shapes=scratch,
        cost_estimate=pl.CostEstimate(flops=1, bytes_accessed=moved, transcendentals=0),
        compiler_params=pltpu.CompilerParams(vmem_limit_bytes=56 * 2**20),
    )(*[array for array, _ in ins], *held)


def weight_gradient(lefts, mine, theirs, start, total, base=None, earlier=()):
    parts, tokens, rows = lefts.shape
    columns = mine.shape[1]
    tile = 1152
    steps = columns // parts // tile
    held = ([] if base is None else [base]) + jax.tree.leaves(earlier)

    def body(lefts_ref, mine_ref, theirs_ref, *refs):
        half = tokens // 2
        value = dot_tn(lefts_ref[0, :half], mine_ref[...])
        refs[-1][...] = (value + dot_tn(lefts_ref[0, half:], theirs_ref[...])).astype(BF)

    return pl.pallas_call(
        body,
        grid=(parts * steps,),
        in_specs=[
            pl.BlockSpec((1, tokens, rows), lambda step: (step // steps, 0, 0)),
            pl.BlockSpec((tokens // 2, tile), lambda step: (0, step)),
            pl.BlockSpec((tokens // 2, tile), lambda step: (0, step)),
        ]
        + [pl.BlockSpec(memory_space=pl.ANY)] * len(held),
        out_specs=pl.BlockSpec((rows, tile), lambda step: (0, step + start // tile)),
        out_shape=jax.ShapeDtypeStruct((rows, total), BF),
        input_output_aliases={} if base is None else {3: 0},
        cost_estimate=pl.CostEstimate(flops=1, bytes_accessed=1, transcendentals=0),
        compiler_params=pltpu.CompilerParams(vmem_limit_bytes=56 * 2**20),
    )(lefts, mine, theirs, *held)


def after(values, *earlier):
    flat, tree = jax.tree.flatten(values)
    held = jax.tree.leaves(earlier)
    outs = pl.pallas_call(
        lambda *refs: None,
        in_specs=[pl.BlockSpec(memory_space=pl.ANY)] * (len(flat) + len(held)),
        out_specs=[pl.BlockSpec(memory_space=pl.ANY)] * len(flat),
        out_shape=[jax.ShapeDtypeStruct(value.shape, value.dtype) for value in flat],
        input_output_aliases={index: index for index in range(len(flat))},
        cost_estimate=pl.CostEstimate(flops=1, bytes_accessed=1, transcendentals=0),
    )(*flat, *held)
    return jax.tree.unflatten(tree, outs)


def swap(value):
    return lax.ppermute(value, "c", [(0, 1), (1, 0)])


def position_index(axis, place, core):
    if axis == "y":
        return ((place % 2) * 2 + core) * 2 + place // 2
    return place * 2 + core


def receive(value, axis, step, mirrored=True):
    pairs = []
    for core in range(2):
        own = -step if mirrored and core == 1 else step
        for place in range(4):
            pairs.append(
                (position_index(axis, (place + own) % 4, core), position_index(axis, place, core))
            )
    return lax.ppermute(value, NAMES[axis], pairs)


def place_of(axis):
    if axis == "y":
        return 2 * lax.axis_index("u") + lax.axis_index("v")
    return lax.axis_index(axis)


def sign_of():
    return 1 - 2 * lax.axis_index("c")


def places(axis):
    here, sign = place_of(axis), sign_of()
    mine = [here, (here + sign) % 4, (here - sign) % 4, (here + 2) % 4]
    return mine, [mine[0], mine[2], mine[1], mine[3]]


def by_place(pieces, spots):
    slots = jnp.arange(4).reshape((4,) + (1,) * pieces[0].ndim)
    out = pieces[3][None]
    for piece, spot in zip(pieces[:3], spots[:3]):
        out = jnp.where(slots == spot, piece[None], out)
    return out


def gather_direct(value, axis):
    return [
        value,
        receive(value, axis, 1),
        receive(value, axis, -1),
        receive(value, axis, 2, False),
    ]


def scatter(pieces, axis, earlier=()):
    own, first, second, far = pieces
    came = [
        receive(first.astype(BF), axis, -1),
        receive(second.astype(BF), axis, 1),
        receive(far.astype(BF), axis, 2, False),
    ]
    if earlier:
        came = after(came, *earlier)
    return own.astype(F32) + sum(piece.astype(F32) for piece in came)


def exchange(blocks, axes):
    return lax.all_to_all(blocks, axes, 0, 0, tiled=True)


def spread(value, axes, count):
    return exchange(jnp.broadcast_to(value[None], (count,) + value.shape), axes)


def exchange_sum(blocks, axes):
    return jnp.sum(exchange(blocks.astype(BF), axes).astype(F32), 0)


def gather_plane(value):
    return lax.all_gather(value, ("z", "x"), axis=0, tiled=True)


def scatter_plane(value, axes=("z", "x")):
    blocks = value.reshape(16, value.shape[0] // 16, value.shape[1])
    return lax.psum_scatter(blocks, axes, scatter_dimension=0, tiled=True)[0]


def pair_one(when_zero, when_one):
    zero = lax.axis_index("c") == 0
    return jnp.concatenate(
        [jnp.where(zero, when_zero, when_one), swap(jnp.where(zero, when_one, when_zero))], -2
    )


def per_device(
    inputs,
    text,
    masked,
    cot,
    norm_gains,
    norm_biases,
    w_qkv,
    w_out,
    w_text,
    w_query,
    w_memory,
    w_cross_out,
    w_up,
    up_bias,
    w_down,
    down_bias,
):
    inputs, text, masked, cot = inputs[0], text[0], masked[0], cot[0]
    tokens, width = inputs.shape
    half_words = text.shape[0]
    wide = w_up.shape[1]
    part = wide // 8
    rows = w_qkv.shape[0]
    text_rows, down_rows = w_text.shape[0], w_down.shape[0]
    scale = HEAD ** (-0.5)
    core = lax.axis_index("c")
    zero = core == 0
    core_word = core.astype(jnp.int32).reshape(1)
    group = ("v", "c", "u")
    inputs_both = jnp.concatenate([inputs, swap(inputs)], 0)

    extra = jnp.concatenate(
        [
            jnp.stack([norm_gains, norm_biases], 1).reshape(6, rows).T,
            up_bias.reshape(rows, -1),
            down_bias[:, None],
        ],
        1,
    )
    extra = jnp.pad(extra, ((0, 0), (0, 128 - extra.shape[1])))
    halves = jnp.stack(
        [
            jnp.concatenate([w_qkv[:, : 2 * width], extra, w_out], 1),
            jnp.concatenate([w_qkv[:, 2 * width :], w_query, extra, w_cross_out], 1),
        ]
    )
    half_columns = halves.shape[-1]
    halves = jnp.broadcast_to(halves[None, :, None], (2, 2, 2) + halves.shape[1:])
    eighths = w_up.reshape(rows, 16, 8, down_rows).transpose(2, 0, 1, 3).reshape(8, rows, part)
    columns = half_columns + WIDE
    words = text.reshape(half_words, 16, 8, text_rows).transpose(2, 0, 1, 3).reshape(8, 2, -1)
    parts = jnp.concatenate(
        [
            jnp.concatenate(
                [
                    halves.reshape(8, rows, half_columns),
                    jnp.pad(eighths, ((0, 0), (0, 0), (0, WIDE - part))),
                ],
                2,
            ),
            jnp.pad(words, ((0, 0), (0, 0), (0, columns - words.shape[2]))),
        ],
        1,
    )
    parts = exchange(parts, group)
    joined_columns = 2 * width + 128
    own = gather_plane(parts[:, :rows, :joined_columns].reshape(8 * rows, joined_columns))
    text_all = parts[:, rows:, : words.shape[2]].reshape(8 * half_words, 16 * text_rows)

    sorted_text = w_text.reshape(text_rows, 16, 8, rows).transpose(0, 2, 1, 3).reshape(text_rows, width)
    slab = jnp.concatenate([sorted_text, w_memory.reshape(2 * rows, width)], 0)
    slab = by_place(gather_direct(slab, "x"), places("x")[0])
    slab = by_place(gather_direct(slab, "z"), places("z")[0]).reshape(16, -1, width)
    text_weight = slab[:, :text_rows].reshape(-1, width)
    memory_weight = slab[:, text_rows:].reshape(16 * rows, 2 * width)

    packed = jnp.concatenate(
        [
            parts[:, :rows, joined_columns:].reshape(8 * rows, width + WIDE),
            jnp.concatenate([w_down[:, :WIDE], w_down[:, width - WIDE :]], 0),
        ],
        1,
    )
    packed = gather_plane(packed)

    def other_half(values):
        return lax.ppermute(values, "u", [(0, 1), (1, 0)])

    def both_cores(ring):
        ring = jnp.concatenate(ring, 0)
        return jnp.concatenate([ring, swap(ring)], 0)

    def fold_tokens(values):
        ring = values[: 4 * tokens] + swap(values[4 * tokens :].astype(BF)).astype(F32)
        return [ring[index * tokens : (index + 1) * tokens] for index in range(4)]

    projected = dot(text_all, text_weight).reshape(8 * half_words, 8, 16 * rows).transpose(1, 0, 2)
    projected = exchange_sum(projected, group).astype(BF)
    loss_tokens = masked.astype(F32)[:, None]
    branch = (cot.astype(F32) * loss_tokens).astype(BF)
    branch_all = both_cores(gather_direct(after(branch, text_all), "y"))
    down_shift_grad = jnp.sum(branch.astype(F32), 0)
    own = after(own, branch_all, projected)
    shifts = own[:, 2 * width : 2 * width + 128].astype(F32)
    norms = shifts[:, :6].T

    first, mine, theirs, own = call(
        project_kernel,
        [(inputs_both, "v"), (norms, "v"), (own, "a")],
        [((2 * tokens, width), BF), ((tokens, 2 * width), BF), ((tokens, 2 * width), BF)],
        [pltpu.VMEM((width, 2 * width), BF), pltpu.SemaphoreType.DMA((1,))],
        handed=2,
    )
    theirs = swap(theirs)
    queries = jnp.where(zero, mine[:, :width], theirs[:, :width])
    key_value = jnp.concatenate(
        [
            jnp.where(zero, mine[:, width:], theirs[:, width:]),
            jnp.where(zero, theirs[:, :width], mine[:, :width]),
        ],
        1,
    )
    own = after(own, key_value)
    other = swap(own)
    key_value = jnp.concatenate([key_value, other_half(key_value)], 0)
    projected = after(projected, key_value)
    words = dot(projected, memory_weight).reshape(4, 1, 2 * half_words, 2 * width)
    words = jnp.broadcast_to(words, (4, 2) + words.shape[2:]).reshape(8, 2 * half_words, 2 * width)
    words = exchange(words.astype(BF), group)
    attended = call(
        functools.partial(attend_kernel, scale),
        [(queries, "v"), (key_value, "v")],
        [((tokens, width), BF)],
        [pltpu.VMEM((tokens, width), F32)],
    )[0]
    packed, words = after((packed, words), attended)
    mixed_own = packed[:, :width]
    words = jnp.sum(words.astype(F32), 0).astype(BF)
    mixed_other = swap(mixed_own)
    weights = [(value, "a") for value in (mixed_own, mixed_other, own, other)]
    second, second_in, cross_queries, cross_out, third, third_in = call(
        functools.partial(forward_kernel, scale),
        [(core_word, "s"), (attended, "v"), (inputs, "v"), (words, "v"), (norms, "v")]
        + weights,
        [
            ((tokens, width), F32),
            ((tokens, width), BF),
            ((tokens, width), BF),
            ((tokens, width), BF),
            ((tokens, width), F32),
            ((tokens, width), BF),
        ],
        [
            pltpu.VMEM((width, width), BF),
            pltpu.VMEM((width, width), BF),
            pltpu.VMEM((width, width), BF),
            pltpu.VMEM((tokens, width), F32),
            pltpu.SemaphoreType.DMA((3,)),
        ],
    )
    shifts = after(shifts, third_in)
    place = (lax.axis_index("v") * 2 + core) * 2 + lax.axis_index("u")
    up_shift = lax.dynamic_index_in_dim(
        shifts[:, 6:10].reshape(16, 8, down_rows), place, 1, False
    ).reshape(part)
    down_shift = shifts[:, 10]
    up_weight, down_weight = call(
        unpack_kernel,
        [(packed, "v")],
        [((width, part), BF), ((part, width), BF)],
        [],
        [third_in],
    )

    third_all = both_cores(gather_direct(third_in, "y"))
    hidden_grad = dot_nt(branch_all, down_weight)
    upward = dot(third_all, up_weight) + up_shift
    upward_grad = jax.vjp(jax.nn.gelu, upward)[1](hidden_grad)[0].astype(BF)
    hidden = jax.nn.gelu(upward).astype(BF)
    third_in_grad = fold_tokens(dot_nt(upward_grad, up_weight))
    up_down_grad = call(
        feed_forward_kernel,
        [(third_all, "v"), (upward_grad, "v"), (hidden, "v"), (branch_all, "v")],
        [((16, 8 * rows, 2 * WIDE), BF)],
        [],
        third_in_grad,
        1,
    )[0]
    third_in_grad = scatter(third_in_grad, "y", [up_down_grad])
    up_down_total = lax.psum_scatter(
        up_down_grad, ("z", "x"), scatter_dimension=0, tiled=True
    )[0].astype(F32)
    up_shift_grad = jnp.sum(upward_grad.astype(F32), 0)

    (
        cross_branch,
        cross_query_grad,
        words_grad,
        self_branch,
        second_grad,
        attended_grad,
        norm_grads,
    ) = call(
        functools.partial(cross_back_kernel, scale),
        [
            (core_word, "s"),
            (third_in_grad, "v"),
            (third, "v"),
            (second, "v"),
            (cot, "v"),
            (loss_tokens, "v"),
            (words, "v"),
            (cross_queries, "v"),
            (norms, "v"),
        ]
        + weights,
        [
            ((tokens, width), BF),
            ((tokens, width), BF),
            ((2 * half_words, 2 * width), BF),
            ((tokens, width), BF),
            ((tokens, width), F32),
            ((tokens, width), BF),
            ((8, width), F32),
        ],
        [
            pltpu.VMEM((width, width), BF),
            pltpu.VMEM((width, width), BF),
            pltpu.VMEM((width, width), BF),
            pltpu.VMEM((tokens, width), BF),
            pltpu.VMEM((tokens, width), F32),
            pltpu.VMEM((2 * half_words, 2 * width), F32),
            pltpu.SemaphoreType.DMA((3,)),
        ],
        [up_down_grad],
    )
    query_grad, key_grad, value_grad, key_value_else = call(
        functools.partial(attend_back_kernel, scale),
        [(queries, "v"), (key_value, "v"), (attended_grad, "v")],
        [
            ((tokens, width), BF),
            ((tokens, width), BF),
            ((tokens, width), BF),
            ((tokens, 2 * width), BF),
        ],
        [pltpu.VMEM((tokens, width), F32), pltpu.VMEM((2 * tokens, 2 * width), F32)],
    )
    words_grad = spread(words_grad, group, 8).reshape(4, 2, 2 * half_words, 2 * width)
    words_grad = jnp.sum(words_grad.astype(F32), 1).reshape(8 * half_words, 2 * width).astype(BF)
    projected_grad = spread(
        dot_nt(after(words_grad, key_value_else), memory_weight).astype(BF), group, 8
    )
    projected_grad = projected_grad.transpose(1, 0, 2).reshape(8 * half_words, width)

    attention_columns = 3 * width
    branch_mine = jnp.where(zero, self_branch, cross_branch)
    branch_theirs = swap(jnp.where(zero, cross_branch, self_branch))
    first_right = jnp.where(zero, first, pair_one(second_in, second_in))
    attention_grad = weight_gradient(
        pair_one(attended, cross_out)[None],
        branch_mine,
        branch_theirs,
        2 * width,
        attention_columns,
        earlier=[key_value_else, first_right],
    )
    key_grad, value_grad, mine, send = call(
        late_kernel,
        [
            (core_word, "s"),
            (query_grad, "v"),
            (key_grad, "v"),
            (value_grad, "v"),
            (other_half(key_value_else), "v"),
            (cross_query_grad, "v"),
        ],
        [((tokens, width), BF)] * 2 + [((tokens, 2 * width), BF)] * 2,
        [],
        [attention_grad],
    )
    attention_grad = weight_gradient(
        jnp.stack([first, first_right]),
        mine,
        swap(send),
        0,
        attention_columns,
        attention_grad,
    )

    input_grads, last_grads = call(
        input_kernel,
        [
            (core_word, "s"),
            (query_grad, "v"),
            (key_grad, "v"),
            (value_grad, "v"),
            (inputs, "v"),
            (second_grad, "v"),
            (norms, "v"),
        ]
        + weights[2:],
        [((tokens, width), F32), ((8, width), F32)],
        [
            pltpu.VMEM((width, 2 * width), BF),
            pltpu.VMEM((width, width), BF),
            pltpu.SemaphoreType.DMA((2,)),
        ],
        [attention_grad],
    )
    projected_grad = after(projected_grad, attention_grad)
    slab_grad = jnp.concatenate(
        [
            dot_tn(text_all, projected_grad).reshape(16, text_rows, width),
            dot_tn(projected, words_grad).reshape(16, 2 * rows, width),
        ],
        1,
    )

    final = third + scatter(
        fold_tokens(dot(after(hidden, attention_grad), down_weight)), "y"
    ) + down_shift
    block_output = final.astype(BF)

    down_total = jnp.concatenate(
        [
            up_down_total[:down_rows, WIDE : WIDE + part],
            up_down_total[down_rows:, WIDE : WIDE + part],
        ],
        1,
    )
    by_place_part = jnp.where(
        jnp.arange(8)[None, :, None] == place, up_shift_grad.reshape(16, 1, down_rows), 0.0
    ).reshape(128, down_rows)
    gain_terms = jnp.concatenate([last_grads[:1], norm_grads[1:3]], 0)
    shift_terms = jnp.concatenate([last_grads[1:2], norm_grads[4:6]], 0)
    small_grads = jnp.concatenate(
        [
            gain_terms.reshape(3, 128, rows).transpose(1, 0, 2).reshape(128, 3 * rows),
            shift_terms.reshape(3, 128, rows).transpose(1, 0, 2).reshape(128, 3 * rows),
            by_place_part,
            down_shift_grad.reshape(128, rows),
        ],
        1,
    )

    def split(values):
        high = values.astype(BF)
        return high, (values - high.astype(F32)).astype(BF)

    count = small_grads.shape[1]
    small_grads = jnp.pad(
        small_grads.reshape(16, 8, count), ((0, 0), (0, 0), (0, 8 * rows * 2 - count))
    ).reshape(16, width)
    slab_grad = jnp.concatenate([slab_grad.astype(BF), jnp.stack(split(small_grads), 1)], 1)
    slab_total = exchange_sum(slab_grad, ("z", "x"))
    text_total = (
        slab_total[:text_rows]
        .reshape(text_rows, 8, 16, rows)
        .transpose(0, 2, 1, 3)
        .reshape(text_rows, width)
    )
    memory_total = slab_total[text_rows:-2].reshape(rows, 2 * width)
    small_total = split(jnp.sum(slab_total[-2:], 0).reshape(8, 1, -1))

    total = scatter_plane(attention_grad).reshape(8, rows, -1)
    total = jnp.concatenate(
        [
            jnp.concatenate([total, up_down_total[:, :WIDE].astype(BF).reshape(8, rows, WIDE)], 2),
            jnp.pad(
                jnp.concatenate(small_total, 2),
                ((0, 0), (0, 0), (0, attention_columns + WIDE - 2 * small_total[0].shape[2])),
            ),
        ],
        1,
    )
    total = exchange(total, group)
    joined_total, query_total, out_total, cross_total_grad = call(
        finish_kernel,
        [(total, "v")],
        [((rows, 3 * width), F32)] + [((rows, width), F32)] * 3,
        [],
    )
    up_total = (
        total[:, :rows, attention_columns : attention_columns + part]
        .reshape(8, rows, 16, down_rows)
        .transpose(1, 2, 0, 3)
        .reshape(rows, wide)
        .astype(F32)
    )
    small_total = jnp.sum(total[:, rows].astype(F32), 0)
    small_total = small_total[:count] + small_total[16 * rows : 16 * rows + count]
    gain_total = small_total[: 3 * rows].reshape(3, rows)
    shift_total = small_total[3 * rows : 6 * rows].reshape(3, rows)
    up_shift_total = small_total[6 * rows : 6 * rows + down_rows]
    down_shift_total = small_total[6 * rows + down_rows :]
    return (
        block_output[None],
        input_grads[None],
        gain_total,
        shift_total,
        joined_total,
        out_total,
        text_total,
        query_total,
        memory_total,
        cross_total_grad,
        up_total,
        up_shift_total,
        down_total,
        down_shift_total,
    )


def solution(mesh):
    fine = Mesh(mesh.devices.reshape(4, 4, 2, 2, 2), AXES)
    tokens = P(DP, "u", None)
    split_rows = P(AXES, None)
    split_columns = P(None, AXES)
    split_vector = P(AXES)
    return jax.shard_map(
        per_device,
        mesh=fine,
        in_specs=(tokens, tokens, P(DP, "u"), tokens)
        + (split_columns,) * 2
        + (split_rows,) * 7
        + (split_vector, split_rows, split_vector),
        out_specs=(tokens, tokens)
        + (split_columns,) * 2
        + (split_rows,) * 7
        + (split_vector, split_rows, split_vector),
        check_vma=False,
    )
```
